128 devices in a mesh: group: 8 (over y, core), tp: 16 (over x, z).
Axes of the slice: x: 4, y: 4, z: 4, core: 2. Of those that a mesh axis runs over, the one named last changes fastest.
Arguments:
- residual: bfloat16 [768, 4096], P('group', 'tp'), may hold values from -18 to 18
- tree_qkv: bfloat16 [3, 768, 4096], P(None, 'group', 'tp'), may hold values from -12.5 to 12.5
- kv_pool: bfloat16 [2, 256, 128, 4096], P(None, 'group', None, 'tp'), may hold values from -12.5 to 12.5
- page_table: int32 [16, 28], replicated, may hold values from 0 to 31, as said below
- cache_len: int32 [16], replicated, may hold values from 1 to 3584, as said below
- tree_parent: int32 [16, 48], replicated, may hold values from 0 to 46, as said below
- accepted_nodes: int32 [16, 4], P('group'), may hold values from 0 to 47
- out_weight: bfloat16 [4096, 4096], P('tp'), may hold values from -0.125 to 0.125
- norm_gain: float32 [4096], P('tp'), may hold values from 0.5 to 1.5
- draft_weight: bfloat16 [3, 4096, 4096], P(None, None, 'tp'), may hold values from -0.09375 to 0.09375
- vocab_weight: bfloat16 [26624, 4096], P('tp'), may hold values from -1.75 to 1.75
- target_ids: int32 [4, 768], P(None, 'group'), may hold values from 0 to 26623
Outputs:
- log_probs: float32 [4, 768], P(None, 'group')
- accepted_kv: bfloat16 [2, 64, 4096], P(None, 'group', 'tp')
The draws below stay inside these ranges and needn't reach their ends.
Inputs may be any that keep to these rules, and one draw needn't show every extreme that they name: `cache_len`: request 2 g is group g's short request and request 2 g + 1 its long one; a short request has at most 512 positions and some group's has exactly that many; a long request has 128 or more and some group's has exactly 3584. `page_table`: entries of request r of group g = r // 2 are slots of group g's pool, except the odd columns of a long request, which are slots of group g xor 1's pool. In each group's pool the short request's first 4 columns, its long request's even columns and the odd columns of group g xor 1's long request are distinct slots covering the pool; a short request's columns from 4 on repeat its first ones. `tree_parent`: node 0 is the root and its own parent; every other node's parent has a smaller index, and node 48 - 1's parent is node 46.
All inputs are finite; a program needn't handle non-finite values.
Results may differ from the reference program's by a relative error of at most 0.004.
Values may be sent and summed in bfloat16 or wider, within the bound.
A program may use at most 128 MiB of HBM per device.

```python
import math
import jax
import jax.numpy as jnp
import numpy as np
from jax import lax

D = 4096
HEADS = 32
HD = 128
VOCAB = 26624
TREE = 48
DRAFTS = 3
ACCEPT = 4
PAGE = 128
HALF_PAGES = 14
SHORT_PAGES = 4
LONG_PAGES = 28
POOL = 32
POOL_ALL = 256
REQS = 16
TOKENS = 768
ROWSETS = 4


def anchor_vector(key):
    base_key = jax.random.fold_in(key, 9001)
    sign_key, size_key = jax.random.split(base_key)
    sign_values = jnp.where(jax.random.bernoulli(sign_key, 0.5, (D,)), 1.0, -1.0)
    magnitude = jax.random.uniform(size_key, (D,), jnp.float32, 13.5, 14.5) / HD ** 0.25
    return sign_values * magnitude


def draw_residual(key, part):
    own_key = jax.random.fold_in(key, 11)
    feature_ramp = jnp.arange(D, dtype=jnp.float32) / D
    values = jnp.clip(jax.random.normal(own_key, (TOKENS, D), jnp.float32), -4.0, 4.0)
    values = values * 0.3 * jnp.power(3.0, feature_ramp)[None, :]
    return values.astype(jnp.bfloat16)


def draw_tree_qkv(key, part):
    own_key = jax.random.fold_in(key, 23)
    values = jnp.clip(jax.random.normal(own_key, (3, TOKENS, D), jnp.float32), -4.0, 4.0)
    anchor = anchor_vector(key)
    token_ids = jnp.arange(TOKENS)
    strength = 0.6 + 0.2 * (token_ids // 8 % 4).astype(jnp.float32)
    aligned = (token_ids % 8 == 0)[:, None]
    queries = jnp.where(aligned, strength[:, None] * anchor[None, :], values[0])
    values = jnp.concatenate([queries[None], values[1:]], 0)
    return values.astype(jnp.bfloat16)


def draw_kv_pool(key, part):
    own_key = jax.random.fold_in(key, 37)
    page_key = jax.random.fold_in(key, 38)
    pool_shape = (2, POOL_ALL, PAGE, D)
    values = jnp.clip(jax.random.normal(own_key, pool_shape, jnp.float32), -4.0, 4.0)
    anchor = anchor_vector(key)
    page_factor = 1.0 + jax.random.uniform(page_key, (POOL_ALL,), jnp.float32, 0.0, 30.0 / 196.0)
    row_index = jnp.arange(PAGE)
    factor = jnp.where(row_index == PAGE - 1, 1.0, 1.0 + 1.5 / 196.0)
    marked = (row_index >= PAGE - 2)[:, None]
    planted = page_factor[:, None, None] * factor[None, :, None] * anchor[None, None, :]
    key_part = jnp.where(marked[None], planted, values[0])
    values = jnp.concatenate([key_part[None], values[1:]], 0)
    return values.astype(jnp.bfloat16)


def draw_vocab_weight(key, part):
    own_key = jax.random.fold_in(key, 41)
    values = jnp.clip(jax.random.normal(own_key, (VOCAB, D), jnp.float32), -4.0, 4.0) / math.sqrt(D)
    values = jnp.clip(values, -1.75, 1.75)
    return values.astype(jnp.bfloat16)


def draw_cache_len(key, part):
    own_key = jax.random.fold_in(key, 53)
    short_key, long_key, pick_key = jax.random.split(own_key, 3)
    group_total = REQS // 2
    short_len = jax.random.randint(short_key, (group_total,), 1, SHORT_PAGES * PAGE + 1)
    long_len = jax.random.randint(long_key, (group_total,), PAGE, LONG_PAGES * PAGE + 1)
    picks = jax.random.randint(pick_key, (2,), 0, group_total)
    group_ids = jnp.arange(group_total)
    short_len = jnp.where(group_ids == picks[0], SHORT_PAGES * PAGE, short_len)
    long_len = jnp.where(group_ids == picks[1], LONG_PAGES * PAGE, long_len)
    return jnp.stack([short_len, long_len], 1).reshape(REQS).astype(jnp.int32)


def draw_page_table(key, part):
    own_key = jax.random.fold_in(key, 67)
    group_total = REQS // 2
    group_keys = jax.random.split(own_key, group_total)
    orders = jax.vmap(lambda single: jax.random.permutation(single, POOL))(group_keys).astype(jnp.int32)
    columns = jnp.arange(LONG_PAGES)
    short_rows = orders[:, columns % SHORT_PAGES]
    partner = jnp.bitwise_xor(jnp.arange(group_total), 1)
    even_rows = orders[:, SHORT_PAGES + columns // 2]
    odd_rows = orders[partner][:, SHORT_PAGES + HALF_PAGES + columns // 2]
    long_rows = jnp.where(columns % 2 == 0, even_rows, odd_rows)
    return jnp.stack([short_rows, long_rows], 1).reshape(REQS, LONG_PAGES).astype(jnp.int32)


def draw_tree_parent(key, part):
    own_key = jax.random.fold_in(key, 79)
    chain_key = jax.random.fold_in(key, 83)
    limits = jnp.maximum(jnp.arange(TREE), 1)
    parents = jax.random.randint(own_key, (REQS, TREE), 0, limits)
    parents = jnp.where(jnp.arange(TREE)[None, :] == TREE - 1, TREE - 2, parents)
    chain_req = jax.random.randint(chain_key, (), 0, REQS)
    chain = jnp.maximum(jnp.arange(TREE) - 1, 0)
    parents = jnp.where(jnp.arange(REQS)[:, None] == chain_req, chain[None, :], parents)
    return parents.astype(jnp.int32)


def touch_ends(entries, stream_key, least, top_value):
    place = [jax.random.randint(jax.random.fold_in(stream_key, axis), (), 0, length) for axis, length in enumerate(entries.shape)]
    widest = entries.shape.index(max(entries.shape))
    beside = place[:widest] + [(place[widest] + 1) % entries.shape[widest]] + place[widest + 1:]
    return entries.at[tuple(place)].set(least).at[tuple(beside)].set(top_value)


def raised(drawn, rng, source, target, shards_of, factor):
    def block_of(position):
        return (jnp.arange(drawn.shape[position]) // (drawn.shape[position] // shards_of)).reshape((-1,) + (1,) * (drawn.ndim - 1 - position))

    one_side = jax.random.permutation(rng, shards_of)[block_of(target)]
    other_side = (block_of(target) + shards_of // 2) % shards_of
    return jnp.where((block_of(source) == one_side) | (block_of(source) == other_side), factor * drawn, drawn)


def steps_of(rng, shape, shards, least, high):
    gain = 1.0
    for position, blocks in shards:
        heights = jax.random.uniform(jax.random.fold_in(jax.random.fold_in(rng, 6), position), (blocks,), jnp.float32, least / len(shards), high / len(shards))
        gain = gain * jnp.repeat(jnp.exp(heights), shape[position] // blocks).reshape((-1,) + (1,) * (len(shape) - 1 - position))
    return gain


def rank_table(count, lean):
    loads = [(1 << 20) // math.isqrt(grade ** lean) + 1 for grade in range(1, count + 1)]
    deviation = 1 + sum(loads) // (1 << 30)
    return np.cumsum(np.array([max(1, weight // deviation) for weight in loads]))


def ranked(key, shape, number_of, slope):
    table = rank_table(number_of, slope)
    lot = jax.random.randint(jax.random.fold_in(key, 1), shape, 0, int(table[number_of - 1]))
    standing = jnp.searchsorted(jnp.asarray(table, jnp.int32), lot, side="right")
    return jax.random.permutation(jax.random.fold_in(key, 2), number_of)[standing].astype(jnp.int32)


def centred(key, dims, deviation, limit, cuts=(), kind=jnp.bfloat16):
    array = deviation * jax.random.normal(key, dims, jnp.float32)
    if cuts:
        array = array * steps_of(key, dims, cuts, -0.22, 0.18)
    return jnp.clip(array, -limit, limit).astype(kind)


def bell_draw_with(key, dims, scale, bound, cuts, heavy, kind=jnp.bfloat16):
    result = scale * jax.random.normal(key, dims, jnp.float32)
    if cuts:
        result = result * steps_of(key, dims, cuts, -0.22, 0.18)
    return jnp.clip(raised(result, jax.random.fold_in(key, 3), *heavy), -bound, bound).astype(kind)


def setup_inputs(seed: int = 0) -> dict:
    keys = jax.random.split(jax.random.key(seed), 13)
    residual = draw_residual(jax.random.fold_in(keys[12], 71), 0)
    tree_qkv = draw_tree_qkv(jax.random.fold_in(keys[12], 71), 0)
    kv_pool = draw_kv_pool(jax.random.fold_in(keys[12], 71), 0)
    page_table = draw_page_table(jax.random.fold_in(keys[12], 71), 0)
    cache_len = draw_cache_len(jax.random.fold_in(keys[12], 71), 0)
    tree_parent = draw_tree_parent(jax.random.fold_in(keys[12], 71), 0)
    accepted_nodes = touch_ends(jax.random.randint(keys[6], (REQS, ACCEPT), 0, TREE), jax.random.fold_in(keys[6], 1), 0, TREE - 1).astype(jnp.int32)
    out_weight = bell_draw_with(keys[7], (D, D), D ** -0.5, 0.125, ((0, 16),), (0, 1, 16, 2.0))
    norm_gain = jnp.clip(1.0 + 0.1 * jax.random.normal(keys[8], (D,), jnp.float32), 0.5, 1.5)
    draft_weight = centred(keys[9], (DRAFTS, D, D), D ** -0.5, 0.09375, ((2, 16),))
    vocab_weight = draw_vocab_weight(jax.random.fold_in(keys[12], 71), 0)
    target_ids = touch_ends(ranked(keys[11], (ROWSETS, TOKENS), VOCAB, 2), jax.random.fold_in(keys[11], 3), 0, VOCAB - 1).astype(jnp.int32)
    return dict(residual=residual, tree_qkv=tree_qkv, kv_pool=kv_pool, page_table=page_table, cache_len=cache_len, tree_parent=tree_parent, accepted_nodes=accepted_nodes, out_weight=out_weight, norm_gain=norm_gain, draft_weight=draft_weight, vocab_weight=vocab_weight, target_ids=target_ids)


EPSILON = 1e-05

def ancestry(parents):
    number = parents.shape[0]
    indices = jnp.arange(number, dtype=jnp.int32)
    linked = ((parents[:, None] == indices[None, :]) & (indices[:, None] > 0)).astype(jnp.float32)
    reached = jnp.minimum(jnp.eye(number, dtype=jnp.float32) + linked, 1.0)
    for sweep_index in range(max(1, number.bit_length())):
        reached = jnp.minimum(jnp.dot(reached, reached, precision=lax.Precision.HIGHEST), 1.0)
    depths = lax.optimization_barrier(jnp.sum(reached, axis=1)) - 1.0
    return (reached, depths)

def slope_values(first, number):
    ordinal = jnp.arange(number, dtype=jnp.float32) + jnp.asarray(first, jnp.float32) + 1.0
    return jnp.exp2(-8.0 * ordinal / HEADS)

def reference(residual, tree_qkv, kv_pool, page_table, cache_len, tree_parent, accepted_nodes, out_weight, norm_gain, draft_weight, vocab_weight, target_ids):
    slopes = slope_values(0.0, HEADS)
    scale_factor = 1.0 / math.sqrt(HD)
    requests = jnp.arange(REQS, dtype=jnp.int32)
    span = LONG_PAGES * PAGE

    def one_request(request):
        home_group = request // 2
        longer = request % 2 == 1
        columns = jnp.arange(LONG_PAGES, dtype=jnp.int32)
        holder = jnp.where(longer & (columns % 2 == 1), jnp.bitwise_xor(home_group, 1), home_group)
        pool_slots = (holder * POOL + page_table[request]).astype(jnp.int32)
        gathered = jnp.take(kv_pool, pool_slots, axis=1)
        cache_keys = gathered[0].reshape(span, HEADS, HD).astype(jnp.float32)
        cache_vals = gathered[1].reshape(span, HEADS, HD).astype(jnp.float32)
        tree_rows = lax.dynamic_slice_in_dim(tree_qkv, (request * TREE).astype(jnp.int32), TREE, 1)
        queries = tree_rows[0].reshape(TREE, HEADS, HD).astype(jnp.float32)
        tree_keys = tree_rows[1].reshape(TREE, HEADS, HD).astype(jnp.float32)
        tree_vals = tree_rows[2].reshape(TREE, HEADS, HD).astype(jnp.float32)
        reached, depths = ancestry(tree_parent[request])
        length = cache_len[request].astype(jnp.float32)
        positions = jnp.arange(span, dtype=jnp.float32)
        query_pos = length + depths
        key_pos = jnp.concatenate([positions, query_pos])
        allowed = jnp.concatenate([jnp.broadcast_to(positions[None, :] < length, (TREE, span)), reached > 0.5], axis=1)
        all_keys = jnp.concatenate([cache_keys, tree_keys], 0)
        all_vals = jnp.concatenate([cache_vals, tree_vals], 0)
        scores = jnp.einsum('thd,lhd->htl', queries, all_keys) * scale_factor
        scores = scores - slopes[:, None, None] * (query_pos[None, :, None] - key_pos[None, None, :])
        row_top = lax.optimization_barrier(jnp.max(jnp.where(allowed[None], scores, -1e+30), axis=2, keepdims=True))
        weights = jnp.where(allowed[None], jnp.exp(scores - row_top), 0.0)
        weight_sum = lax.optimization_barrier(jnp.sum(weights, axis=2))
        weighted = jnp.einsum('htl,lhd->thd', weights, all_vals, precision=lax.Precision.HIGHEST)
        return (weighted / jnp.transpose(weight_sum)[:, :, None]).reshape(TREE, D).astype(jnp.bfloat16)
    attn = lax.map(one_request, requests).reshape(TOKENS, D)
    head_out = jnp.dot(attn, out_weight, preferred_element_type=jnp.float32)
    hidden = residual.astype(jnp.float32) + head_out
    row_mean = lax.optimization_barrier(jnp.sum(hidden, axis=1, keepdims=True)) / D
    row_var = lax.optimization_barrier(jnp.sum(hidden * hidden, axis=1, keepdims=True)) / D - row_mean * row_mean
    normed = ((hidden - row_mean) * lax.rsqrt(row_var + EPSILON) * norm_gain).astype(jnp.bfloat16)
    drafted = []
    for draft_index in range(DRAFTS):
        update = jnp.dot(normed, draft_weight[draft_index], preferred_element_type=jnp.float32)
        drafted.append((normed.astype(jnp.float32) + jax.nn.silu(update)).astype(jnp.bfloat16))
    stacked = jnp.stack([normed] + drafted)

    def head_probs(paired):
        rowset, targets = paired
        logits = jnp.dot(rowset, vocab_weight.T, preferred_element_type=jnp.float32)
        normalizer = jax.nn.logsumexp(logits, axis=1)
        picked = jnp.take_along_axis(logits, targets[:, None], axis=1)[:, 0]
        return picked - normalizer
    log_probs = lax.map(head_probs, (stacked, target_ids))
    flat_index = (requests[:, None] * TREE + accepted_nodes).reshape(-1).astype(jnp.int32)
    accepted_kv = jnp.take(tree_qkv[1:3], flat_index, axis=1)
    return (log_probs, accepted_kv)
```

```python
import functools
import math

import jax
import jax.numpy as jnp
from jax import lax
from jax.experimental import pallas as pl
from jax.experimental.pallas import tpu as pltpu
from jax.sharding import PartitionSpec as P

D = 4096
HEADS = 32
HD = 128
TREE = 48
SHORT_PAGES = 4
HALF = 14
PAGE = 128
DRAFTS = 3
EPSILON = 1e-05
F32 = jnp.float32
BF16 = jnp.bfloat16
MESH = pl.DeviceIdType.MESH
NT = (((1,), (1,)), ((), ()))


def dot(a, b):
    return jnp.dot(a, b, preferred_element_type=F32)


def dot_nt(a, b):
    return lax.dot_general(a, b, NT, preferred_element_type=F32)


def both_heads(rows):
    lane = lax.broadcasted_iota(jnp.int32, rows.shape, 1)
    zero = jnp.zeros_like(rows)
    return jnp.concatenate(
        [jnp.where(lane < HD, rows, zero), jnp.where(lane >= HD, rows, zero)], axis=0
    )


def own_heads(stacked):
    n = stacked.shape[0] // 2
    return jnp.concatenate([stacked[:n, :HD], stacked[n:, HD:]], axis=1)


def wide(column):
    n = column.shape[0] // 2
    return jnp.concatenate(
        [jnp.broadcast_to(column[:n], (n, HD)), jnp.broadcast_to(column[n:], (n, HD))], axis=1
    )


def row_slopes(lane_index, rows):
    second = lax.broadcasted_iota(jnp.int32, (rows, 1), 0) >= rows // 2
    ordinal = (lane_index * 2 + 1 + jnp.where(second, 1, 0)).astype(F32)
    return jnp.exp2(-8.0 * ordinal / HEADS)


def cache_part(queries, keys, values, slopes, length, first, stride):
    span = keys.shape[0]
    scores = dot_nt(queries, keys) * (1.0 / math.sqrt(HD))
    index = lax.broadcasted_iota(jnp.int32, (1, span), 1)
    place = ((index >> 7) * stride + first) * PAGE + (index & (PAGE - 1))
    relative = place.astype(F32) - length
    exists = relative < 0.0
    scores = jnp.where(exists, scores + slopes * relative, -1e30)
    top = jnp.max(scores, axis=1, keepdims=True)
    weights = jnp.where(exists, jnp.exp(scores - top), 0.0)
    total = jnp.sum(weights, axis=1, keepdims=True)
    return top, total, own_heads(dot(weights.astype(BF16), values))


def join(one, two):
    top = jnp.maximum(one[0], two[0])
    f1, f2 = jnp.exp(one[0] - top), jnp.exp(two[0] - top)
    return top, one[1] * f1 + two[1] * f2, one[2] * wide(f1) + two[2] * wide(f2)


def kernel(
    ntp,
    residual,
    tree,
    pool,
    pages,
    lens,
    parents,
    accepted,
    out_w,
    gain,
    draft_w,
    vocab_w,
    targets,
    probs_out,
    kept_out,
    kbank,
    vbank,
    kbuf,
    vbuf,
    ow,
    dw,
    vw,
    guest_q,
    part_o,
    part_s,
    back_o,
    back_s,
    rs_send,
    rs_got,
    rows_got,
    stat_got,
    normed,
    draft_got,
    logits,
    fin_got,
    square,
    hbm_sem,
    pair_send,
    pair_recv,
    rs_ssem,
    rs_rsem,
    rows_ssem,
    rows_rsem,
    stat_ssem,
    stat_rsem,
    draft_ssem,
    draft_rsem,
    fin_ssem,
    fin_rsem,
):
    g = lax.axis_index("group")
    me = lax.axis_index("tp")
    partner = g + 1 - 2 * lax.rem(g, 2)
    tokens, width = residual.shape
    vocab = vw.shape[0]

    def peer(p):
        return lax.rem(me + p, ntp)

    def cols(t):
        return pl.ds(pl.multiple_of(t * width, width), width)

    def to(src, dst, ssem, rsem, where):
        return pltpu.make_async_remote_copy(
            src_ref=src, dst_ref=dst, send_sem=ssem, recv_sem=rsem, device_id=where, device_id_type=MESH
        )

    def load(src, dst, k):
        return pltpu.make_async_copy(src, dst, hbm_sem.at[k])

    load_k = load(pool.at[0], kbank, 0)
    load_v = load(pool.at[1], vbank, 1)
    load_o = load(out_w, ow, 2)
    load_d = load(draft_w, dw, 3)
    load_w = load(vocab_w, vw, 4)
    load_k.start()
    load_v.start()

    barrier = pltpu.get_barrier_semaphore()
    pl.semaphore_signal(barrier, inc=1, device_id=(partner, me), device_id_type=MESH)

    @pl.loop(1, ntp)
    def _(p):
        pl.semaphore_signal(barrier, inc=1, device_id=(g, peer(p)), device_id_type=MESH)

    parent = parents[pl.ds(g, 1), :]
    sub = lax.broadcasted_iota(jnp.int32, (tokens, tokens), 0)
    lan = lax.broadcasted_iota(jnp.int32, (tokens, tokens), 1)
    base = jnp.where(lan >= TREE, TREE, 0)
    linked = (parent + base == sub) & (lan != base)
    up = jnp.where(linked | (sub == lan), 1.0, 0.0).astype(BF16)
    for _ in range(TREE.bit_length()):
        up = jnp.minimum(dot(up, up), 1.0).astype(BF16)
    up32 = up.astype(F32)
    depth = jnp.sum(up32, axis=0, keepdims=True) - 1.0
    square[...] = jnp.zeros_like(square)
    square[0:tokens, 0:tokens] = up32
    ancestor = square[...].T[0:tokens, 0:tokens]

    row = lax.broadcasted_iota(jnp.int32, (16, tokens), 0)
    col = lax.broadcasted_iota(jnp.int32, (16, tokens), 1)
    pick = jnp.zeros((16, tokens), jnp.bool_)
    for i in range(8):
        pick = pick | ((row == i) & (col == (i // 4) * TREE + accepted[i // 4, i % 4]))
    chosen = jnp.where(pick, 1.0, 0.0).astype(BF16)
    for c in range(2):
        kept_out[c] = dot(chosen, tree[c + 1])[0:8].astype(BF16)

    pl.semaphore_wait(barrier, ntp)
    ask = to(tree.at[0, pl.ds(TREE, TREE)], guest_q, pair_send.at[0], pair_recv.at[0], (partner, me))
    ask.start()

    slopes = row_slopes(me, 2 * TREE)
    mine, guest = 2 * g + 1, 2 * partner + 1

    load_k.wait()
    load_o.start()
    load_d.start()

    def collect(bank, buf):
        for start, count, request, first, stride in (
            (0, HALF, guest, 1, 2),
            (HALF, HALF, mine, 0, 2),
            (2 * HALF, SHORT_PAGES, 2 * g, 0, 1),
        ):

            @pl.loop(0, count)
            def _(i):
                buf[pl.ds(pl.multiple_of((start + i) * PAGE, PAGE), PAGE), :] = bank[
                    pages[request, first + stride * i]
                ]

    collect(kbank, kbuf)
    load_v.wait()
    load_w.start()
    collect(vbank, vbuf)

    def over(first, count):
        return pl.ds(first * PAGE, count * PAGE)

    ask.wait_recv()
    top, total, out = cache_part(
        both_heads(guest_q[...]),
        kbuf[over(0, HALF)],
        vbuf[over(0, HALF)],
        slopes,
        lens[guest].astype(F32),
        1,
        2,
    )
    part_o[...] = out
    lane = lax.broadcasted_iota(jnp.int32, (2 * TREE, 128), 1)
    part_s[...] = jnp.where(lane < 64, top, total)
    give_o = to(part_o, back_o, pair_send.at[1], pair_recv.at[1], (partner, me))
    give_s = to(part_s, back_s, pair_send.at[2], pair_recv.at[2], (partner, me))
    give_o.start()
    give_s.start()

    long_part = cache_part(
        both_heads(tree[0, TREE : 2 * TREE]),
        kbuf[over(HALF, HALF)],
        vbuf[over(HALF, HALF)],
        slopes,
        lens[mine].astype(F32),
        0,
        2,
    )
    short_part = cache_part(
        both_heads(tree[0, 0:TREE]),
        kbuf[over(2 * HALF, SHORT_PAGES)],
        vbuf[over(2 * HALF, SHORT_PAGES)],
        slopes,
        lens[2 * g].astype(F32),
        0,
        1,
    )

    seen = jnp.concatenate([ancestor, ancestor], axis=0) > 0.5
    scores = dot_nt(both_heads(tree[0]), tree[1]) * (1.0 / math.sqrt(HD))
    scores = jnp.where(seen, scores + row_slopes(me, 2 * tokens) * depth, -1e30)
    top = jnp.max(scores, axis=1, keepdims=True)
    weights = jnp.where(seen, jnp.exp(scores - top), 0.0)
    total = jnp.sum(weights, axis=1, keepdims=True)
    out = own_heads(dot(weights.astype(BF16), tree[2]))

    def of_request(r):
        at = r * TREE
        return (
            jnp.concatenate([top[at : at + TREE], top[tokens + at : tokens + at + TREE]], 0),
            jnp.concatenate([total[at : at + TREE], total[tokens + at : tokens + at + TREE]], 0),
            out[at : at + TREE],
        )

    short = join(of_request(0), short_part)
    long = join(of_request(1), long_part)
    give_o.wait_recv()
    give_s.wait_recv()
    back = back_s[...]
    long = join(long, (back[:, 0:1], back[:, 64:65], back_o[...]))
    attn = jnp.concatenate([short[2] / wide(short[1]), long[2] / wide(long[1])], 0).astype(BF16)

    load_o.wait()

    @pl.loop(1, ntp)
    def _(p):
        t = peer(p)
        rs_send[t] = dot(attn, ow[:, cols(t)]).astype(BF16)
        to(rs_send.at[t], rs_got.at[me], rs_ssem.at[t], rs_rsem.at[me], (g, t)).start()

    hidden = residual[...].astype(F32) + dot(attn, ow[:, cols(me)])

    def add_share(p, so_far):
        s = peer(p)
        to(rs_send.at[s], rs_got.at[s], rs_ssem.at[s], rs_rsem.at[s], (g, s)).wait_recv()
        return so_far + rs_got[s].astype(F32)

    hidden = lax.fori_loop(1, ntp, add_share, hidden)

    block_sum = jnp.sum(hidden, axis=1, keepdims=True)
    block_square = jnp.sum(hidden * hidden, axis=1, keepdims=True)
    block_mean = block_sum * (1.0 / width)
    rows_got[me] = (hidden - block_mean).astype(BF16)
    lane = lax.broadcasted_iota(jnp.int32, (tokens, 128), 1)
    square[0:tokens, :] = jnp.where(
        lane == 0, block_sum, jnp.where(lane == 1, block_square, jnp.where(lane == 2, block_mean, 0.0))
    )
    stat_got[me] = square[...].T[0:8]
    stat_got[me, 4:6, :] = gain[...]

    @pl.loop(1, ntp)
    def _(p):
        t = peer(p)
        to(stat_got.at[me], stat_got.at[me], stat_ssem.at[t], stat_rsem.at[me], (g, t)).start()
        to(rows_got.at[me], rows_got.at[me], rows_ssem.at[t], rows_rsem.at[me], (g, t)).start()

    @pl.loop(1, ntp)
    def _(p):
        s = peer(p)
        to(stat_got.at[s], stat_got.at[s], stat_ssem.at[s], stat_rsem.at[s], (g, s)).wait_recv()
        to(rows_got.at[s], rows_got.at[s], rows_ssem.at[s], rows_rsem.at[s], (g, s)).wait_recv()

    stats = stat_got[...].reshape(128, 128).T[0:tokens]
    mean = jnp.sum(jnp.where(lane % 8 == 0, stats, 0.0), axis=1, keepdims=True) * (1.0 / D)
    spread = jnp.sum(jnp.where(lane % 8 == 1, stats, 0.0), axis=1, keepdims=True) * (1.0 / D)
    scale = lax.rsqrt(spread - mean * mean + EPSILON)
    for s in range(ntp):
        shift = stats[:, 8 * s + 2 : 8 * s + 3] - mean
        gains = jnp.concatenate([stat_got[s, 4:5, :], stat_got[s, 5:6, :]], axis=1)
        normed[:, s * width : (s + 1) * width] = (
            (rows_got[s].astype(F32) + shift) * scale * gains
        ).astype(BF16)

    load_d.wait()
    own_rows = normed[:, cols(me)].astype(F32)
    for k in range(DRAFTS):
        update = dot(normed[...], dw[k])
        draft_got[k, :, cols(me)] = (own_rows + update / (1.0 + jnp.exp(-update))).astype(BF16)

        @pl.loop(1, ntp)
        def _(p):
            t = peer(p)
            here = draft_got.at[k, :, cols(me)]
            to(here, here, draft_ssem.at[k, t], draft_rsem.at[k, me], (g, t)).start()

    load_w.wait()
    step = 256
    whole = vocab // step

    def some_logits(rows, first):
        def block(at, n):
            logits[first : first + rows.shape[0], pl.ds(at, n)] = dot_nt(rows, vw[pl.ds(at, n), :])

        @pl.loop(0, whole)
        def _(i):
            block(pl.multiple_of(i * step, step), step)

        if vocab > whole * step:
            block(whole * step, vocab - whole * step)

    some_logits(normed[...], 0)

    square[...] = jnp.zeros_like(square)
    square[0:4, 0:tokens] = targets[...].astype(F32)
    wanted = square[...].T[0:tokens]

    for k in range(DRAFTS):

        @pl.loop(1, ntp)
        def _(p):
            s = peer(p)
            there = draft_got.at[k, :, cols(s)]
            to(there, there, draft_ssem.at[k, s], draft_rsem.at[k, s], (g, s)).wait_recv()

    some_logits(draft_got[...].reshape(DRAFTS * tokens, D), tokens)

    entry = (lax.broadcasted_iota(jnp.int32, (1, vocab), 1) + me * vocab).astype(F32)
    summary = jnp.zeros((tokens, 128), F32)
    for k in range(DRAFTS + 1):
        x = logits[k * tokens : (k + 1) * tokens, :]
        top = jnp.max(x, axis=1, keepdims=True)
        total = jnp.sum(jnp.exp(x - top), axis=1, keepdims=True)
        picked = jnp.sum(jnp.where(entry == wanted[:, k : k + 1], x, 0.0), axis=1, keepdims=True)
        for c, value in enumerate((top, total, picked)):
            summary = jnp.where(lane == 8 * c + k, value, summary)
    square[0:tokens, :] = summary
    fin_got[me] = square[...].T[0:24]

    @pl.loop(1, ntp)
    def _(p):
        t = peer(p)
        to(fin_got.at[me], fin_got.at[me], fin_ssem.at[t], fin_rsem.at[me], (g, t)).start()

    ask.wait_send()
    give_o.wait_send()
    give_s.wait_send()

    @pl.loop(1, ntp)
    def _(p):
        t = peer(p)
        to(rs_send.at[t], rs_got.at[me], rs_ssem.at[t], rs_rsem.at[me], (g, t)).wait_send()
        to(stat_got.at[me], stat_got.at[me], stat_ssem.at[t], stat_rsem.at[me], (g, t)).wait_send()
        to(rows_got.at[me], rows_got.at[me], rows_ssem.at[t], rows_rsem.at[me], (g, t)).wait_send()
        for k in range(DRAFTS):
            here = draft_got.at[k, :, cols(me)]
            to(here, here, draft_ssem.at[k, t], draft_rsem.at[k, me], (g, t)).wait_send()

    @pl.loop(1, ntp)
    def _(p):
        s = peer(p)
        to(fin_got.at[s], fin_got.at[s], fin_ssem.at[s], fin_rsem.at[s], (g, s)).wait_recv()

    tops, totals, picks = fin_got[:, 0:8, :], fin_got[:, 8:16, :], fin_got[:, 16:24, :]
    top = jnp.max(tops, axis=0)
    total = jnp.sum(totals * jnp.exp(tops - top[None]), axis=0)
    answer = jnp.sum(picks, axis=0) - (top + jnp.log(total))
    probs_out[...] = answer[0:4, 0:tokens]

    @pl.loop(1, ntp)
    def _(p):
        t = peer(p)
        to(fin_got.at[me], fin_got.at[me], fin_ssem.at[t], fin_rsem.at[me], (g, t)).wait_send()


def shards(ntp, *args):
    (
        residual,
        tree_qkv,
        kv_pool,
        page_table,
        cache_len,
        tree_parent,
        accepted_nodes,
        out_weight,
        norm_gain,
        draft_weight,
        vocab_weight,
        target_ids,
    ) = args
    tokens, width = residual.shape
    slots = kv_pool.shape[1]
    used = (2 * HALF + SHORT_PAGES) * PAGE
    vmem = pl.BlockSpec(memory_space=pltpu.VMEM)
    smem = pl.BlockSpec(memory_space=pltpu.SMEM)
    anywhere = pl.BlockSpec(memory_space=pl.ANY)
    dma = pltpu.SemaphoreType.DMA
    return pl.pallas_call(
        functools.partial(kernel, ntp),
        out_shape=(
            jax.ShapeDtypeStruct((DRAFTS + 1, tokens), F32),
            jax.ShapeDtypeStruct((2, 8, width), BF16),
        ),
        in_specs=[vmem, vmem, anywhere, smem, smem, vmem, smem, anywhere, vmem, anywhere, anywhere, vmem],
        out_specs=(vmem, vmem),
        scratch_shapes=[
            pltpu.VMEM((slots, PAGE, width), BF16),
            pltpu.VMEM((slots, PAGE, width), BF16),
            pltpu.VMEM((used, width), BF16),
            pltpu.VMEM((used, width), BF16),
            pltpu.VMEM((width, D), BF16),
            pltpu.VMEM((DRAFTS, D, width), BF16),
            pltpu.VMEM(vocab_weight.shape, BF16),
            pltpu.VMEM((TREE, width), BF16),
            pltpu.VMEM((TREE, width), F32),
            pltpu.VMEM((2 * TREE, 128), F32),
            pltpu.VMEM((TREE, width), F32),
            pltpu.VMEM((2 * TREE, 128), F32),
            pltpu.VMEM((ntp, tokens, width), BF16),
            pltpu.VMEM((ntp, tokens, width), BF16),
            pltpu.VMEM((ntp, tokens, width), BF16),
            pltpu.VMEM((ntp, 8, 128), F32),
            pltpu.VMEM((tokens, D), BF16),
            pltpu.VMEM((DRAFTS, tokens, D), BF16),
            pltpu.VMEM(((DRAFTS + 1) * tokens, vocab_weight.shape[0]), F32),
            pltpu.VMEM((ntp, 24, 128), F32),
            pltpu.VMEM((128, 128), F32),
            dma((5,)),
            dma((3,)),
            dma((3,)),
            dma((ntp,)),
            dma((ntp,)),
            dma((ntp,)),
            dma((ntp,)),
            dma((ntp,)),
            dma((ntp,)),
            dma((DRAFTS, ntp)),
            dma((DRAFTS, ntp)),
            dma((ntp,)),
            dma((ntp,)),
        ],
        compiler_params=pltpu.CompilerParams(
            collective_id=0, has_side_effects=True, vmem_limit_bytes=60 * 1024 * 1024
        ),
        cost_estimate=pl.CostEstimate(flops=6_200_000_000, bytes_accessed=27_000_000, transcendentals=1_000_000),
    )(
        residual,
        tree_qkv,
        kv_pool,
        page_table,
        cache_len,
        tree_parent.reshape(-1, 2 * TREE),
        accepted_nodes,
        out_weight,
        norm_gain.reshape(2, width // 2),
        draft_weight,
        vocab_weight,
        target_ids,
    )


def solution(mesh):
    placed = (
        P("group", "tp"),
        P(None, "group", "tp"),
        P(None, "group", None, "tp"),
        P(),
        P(),
        P(),
        P("group", None),
        P("tp", None),
        P("tp"),
        P(None, None, "tp"),
        P("tp", None),
        P(None, "group"),
    )
    return jax.shard_map(
        functools.partial(shards, mesh.shape["tp"]),
        mesh=mesh,
        in_specs=placed,
        out_specs=(P(None, "group"), P(None, "group", "tp")),
        check_vma=False,
    )
```

```python
import functools
import math

import jax
import jax.numpy as jnp
from jax import lax
from jax.experimental import pallas as pl
from jax.experimental.pallas import tpu as pltpu
from jax.sharding import PartitionSpec as P

D = 4096
HEADS = 32
HD = 128
TREE = 48
SHORT_PAGES = 4
HALF = 14
PAGE = 128
DRAFTS = 3
EPSILON = 1e-05
F32 = jnp.float32
BF16 = jnp.bfloat16
MESH = pl.DeviceIdType.MESH
NT = (((1,), (1,)), ((), ()))


def dot(a, b):
    return jnp.dot(a, b, preferred_element_type=F32)


def dot_nt(a, b):
    return lax.dot_general(a, b, NT, preferred_element_type=F32)


def both_heads(rows):
    lane = lax.broadcasted_iota(jnp.int32, rows.shape, 1)
    zero = jnp.zeros_like(rows)
    return jnp.concatenate(
        [jnp.where(lane < HD, rows, zero), jnp.where(lane >= HD, rows, zero)], axis=0
    )


def own_heads(stacked):
    n = stacked.shape[0] // 2
    return jnp.concatenate([stacked[:n, :HD], stacked[n:, HD:]], axis=1)


def wide(column):
    n = column.shape[0] // 2
    return jnp.concatenate(
        [jnp.broadcast_to(column[:n], (n, HD)), jnp.broadcast_to(column[n:], (n, HD))], axis=1
    )


def row_slopes(lane_index, rows):
    second = lax.broadcasted_iota(jnp.int32, (rows, 1), 0) >= rows // 2
    ordinal = (lane_index * 2 + 1 + jnp.where(second, 1, 0)).astype(F32)
    return jnp.exp2(-8.0 * ordinal / HEADS)


def cache_part(queries, keys, values, slopes, length, first, stride):
    span = keys.shape[0]
    scores = dot_nt(queries, keys) * (1.0 / math.sqrt(HD))
    index = lax.broadcasted_iota(jnp.int32, (1, span), 1)
    place = ((index >> 7) * stride + first) * PAGE + (index & (PAGE - 1))
    relative = place.astype(F32) - length
    exists = relative < 0.0
    scores = jnp.where(exists, scores + slopes * relative, -1e30)
    top = jnp.max(scores, axis=1, keepdims=True)
    weights = jnp.where(exists, jnp.exp(scores - top), 0.0)
    total = jnp.sum(weights, axis=1, keepdims=True)
    return top, total, own_heads(dot(weights.astype(BF16), values))


def join(one, two):
    top = jnp.maximum(one[0], two[0])
    f1, f2 = jnp.exp(one[0] - top), jnp.exp(two[0] - top)
    return top, one[1] * f1 + two[1] * f2, one[2] * wide(f1) + two[2] * wide(f2)


def kernel(
    ntp,
    residual,
    tree,
    pool,
    pages,
    lens,
    parents,
    accepted,
    out_w,
    gain,
    draft_w,
    vocab_w,
    targets,
    probs_out,
    kept_out,
    kbank,
    vbank,
    kbuf,
    vbuf,
    ow,
    dw,
    vw,
    guest_q,
    part_o,
    part_s,
    back_o,
    back_s,
    rs_send,
    rs_got,
    rows_got,
    stat_got,
    normed,
    draft_got,
    logits,
    fin_got,
    square,
    hbm_sem,
    pair_send,
    pair_recv,
    rs_ssem,
    rs_rsem,
    rows_ssem,
    rows_rsem,
    stat_ssem,
    stat_rsem,
    draft_ssem,
    draft_rsem,
    fin_ssem,
    fin_rsem,
):
    g = lax.axis_index("group")
    me = lax.axis_index("tp")
    partner = g + 1 - 2 * lax.rem(g, 2)
    tokens, width = residual.shape
    vocab = vw.shape[0]

    def peer(p):
        return lax.rem(me + p, ntp)

    def cols(t):
        return pl.ds(pl.multiple_of(t * width, width), width)

    side = math.isqrt(ntp)
    mx, mz = me // side, lax.rem(me, side)

    def hop(axis, by):
        if axis == 0:
            return (g, lax.rem(mx + by, side) * side + mz)
        return (g, mx * side + lax.rem(mz + by, side))

    def to(src, dst, ssem, rsem, where):
        return pltpu.make_async_remote_copy(
            src_ref=src, dst_ref=dst, send_sem=ssem, recv_sem=rsem, device_id=where, device_id_type=MESH
        )

    def load(src, dst, k):
        return pltpu.make_async_copy(src, dst, hbm_sem.at[k])

    load_k = load(pool.at[0], kbank, 0)
    load_v = load(pool.at[1], vbank, 1)
    load_o = load(out_w, ow, 2)
    load_d = load(draft_w, dw, 3)
    load_w = load(vocab_w, vw, 4)
    load_k.start()
    load_v.start()

    barrier = pltpu.get_barrier_semaphore()
    pl.semaphore_signal(barrier, inc=1, device_id=(partner, me), device_id_type=MESH)

    @pl.loop(1, ntp)
    def _(p):
        pl.semaphore_signal(barrier, inc=1, device_id=(g, peer(p)), device_id_type=MESH)

    parent = jnp.concatenate([parents[pl.ds(2 * g, 1), :], parents[pl.ds(2 * g + 1, 1), :]], axis=1)
    sub = lax.broadcasted_iota(jnp.int32, (tokens, tokens), 0)
    lan = lax.broadcasted_iota(jnp.int32, (tokens, tokens), 1)
    base = jnp.where(lan >= TREE, TREE, 0)
    linked = (parent + base == sub) & (lan != base)
    up = jnp.where(linked | (sub == lan), 1.0, 0.0).astype(BF16)
    for _ in range(TREE.bit_length()):
        up = jnp.minimum(dot(up, up), 1.0).astype(BF16)
    up32 = up.astype(F32)
    depth = jnp.sum(up32, axis=0, keepdims=True) - 1.0
    square[...] = jnp.zeros_like(square)
    square[0:tokens, 0:tokens] = up32
    ancestor = square[...].T[0:tokens, 0:tokens]

    row = lax.broadcasted_iota(jnp.int32, (16, tokens), 0)
    col = lax.broadcasted_iota(jnp.int32, (16, tokens), 1)
    pick = jnp.zeros((16, tokens), jnp.bool_)
    for i in range(8):
        pick = pick | ((row == i) & (col == (i // 4) * TREE + accepted[i // 4, i % 4]))
    chosen = jnp.where(pick, 1.0, 0.0).astype(BF16)
    for c in range(2):
        kept_out[c] = dot(chosen, tree[c + 1])[0:8].astype(BF16)

    pl.semaphore_wait(barrier, ntp)
    ask = to(tree.at[0, pl.ds(TREE, TREE)], guest_q, pair_send.at[0], pair_recv.at[0], (partner, me))
    ask.start()

    slopes = row_slopes(me, 2 * TREE)
    mine, guest = 2 * g + 1, 2 * partner + 1

    load_k.wait()
    load_o.start()
    load_d.start()

    def collect(bank, buf):
        for start, count, request, first, stride in (
            (0, HALF, guest, 1, 2),
            (HALF, HALF, mine, 0, 2),
            (2 * HALF, SHORT_PAGES, 2 * g, 0, 1),
        ):

            @pl.loop(0, count)
            def _(i):
                buf[pl.ds(pl.multiple_of((start + i) * PAGE, PAGE), PAGE), :] = bank[
                    pages[request, first + stride * i]
                ]

    collect(kbank, kbuf)
    load_v.wait()
    load_w.start()
    collect(vbank, vbuf)

    def over(first, count):
        return pl.ds(first * PAGE, count * PAGE)

    ask.wait_recv()
    top, total, out = cache_part(
        both_heads(guest_q[...]),
        kbuf[over(0, HALF)],
        vbuf[over(0, HALF)],
        slopes,
        lens[guest].astype(F32),
        1,
        2,
    )
    part_o[...] = out
    lane = lax.broadcasted_iota(jnp.int32, (2 * TREE, 128), 1)
    part_s[...] = jnp.where(lane < 64, top, total)
    give_o = to(part_o, back_o, pair_send.at[1], pair_recv.at[1], (partner, me))
    give_s = to(part_s, back_s, pair_send.at[2], pair_recv.at[2], (partner, me))
    give_o.start()
    give_s.start()

    long_part = cache_part(
        both_heads(tree[0, TREE : 2 * TREE]),
        kbuf[over(HALF, HALF)],
        vbuf[over(HALF, HALF)],
        slopes,
        lens[mine].astype(F32),
        0,
        2,
    )
    short_part = cache_part(
        both_heads(tree[0, 0:TREE]),
        kbuf[over(2 * HALF, SHORT_PAGES)],
        vbuf[over(2 * HALF, SHORT_PAGES)],
        slopes,
        lens[2 * g].astype(F32),
        0,
        1,
    )

    seen = jnp.concatenate([ancestor, ancestor], axis=0) > 0.5
    scores = dot_nt(both_heads(tree[0]), tree[1]) * (1.0 / math.sqrt(HD))
    scores = jnp.where(seen, scores + row_slopes(me, 2 * tokens) * depth, -1e30)
    top = jnp.max(scores, axis=1, keepdims=True)
    weights = jnp.where(seen, jnp.exp(scores - top), 0.0)
    total = jnp.sum(weights, axis=1, keepdims=True)
    out = own_heads(dot(weights.astype(BF16), tree[2]))

    def of_request(r):
        at = r * TREE
        return (
            jnp.concatenate([top[at : at + TREE], top[tokens + at : tokens + at + TREE]], 0),
            jnp.concatenate([total[at : at + TREE], total[tokens + at : tokens + at + TREE]], 0),
            out[at : at + TREE],
        )

    short = join(of_request(0), short_part)
    long = join(of_request(1), long_part)
    give_o.wait_recv()
    give_s.wait_recv()
    back = back_s[...]
    long = join(long, (back[:, 0:1], back[:, 64:65], back_o[...]))
    attn = jnp.concatenate([short[2] / wide(short[1]), long[2] / wide(long[1])], 0).astype(BF16)

    load_o.wait()

    @pl.loop(1, ntp)
    def _(p):
        t = peer(p)
        rs_send[t] = dot(attn, ow[:, cols(t)]).astype(BF16)
        to(rs_send.at[t], rs_got.at[me], rs_ssem.at[t], rs_rsem.at[me], (g, t)).start()

    hidden = residual[...].astype(F32) + dot(attn, ow[:, cols(me)])

    def add_share(p, so_far):
        s = peer(p)
        to(rs_send.at[s], rs_got.at[s], rs_ssem.at[s], rs_rsem.at[s], (g, s)).wait_recv()
        return so_far + rs_got[s].astype(F32)

    hidden = lax.fori_loop(1, ntp, add_share, hidden)

    block_sum = jnp.sum(hidden, axis=1, keepdims=True)
    block_square = jnp.sum(hidden * hidden, axis=1, keepdims=True)
    block_mean = block_sum * (1.0 / width)
    rows_got[me] = (hidden - block_mean).astype(BF16)
    lane = lax.broadcasted_iota(jnp.int32, (tokens, 128), 1)
    square[0:tokens, :] = jnp.where(
        lane == 0, block_sum, jnp.where(lane == 1, block_square, jnp.where(lane == 2, block_mean, 0.0))
    )
    stat_got[me] = square[...].T[0:8]
    stat_got[me, 4:6, :] = gain[...]

    @pl.loop(1, ntp)
    def _(p):
        t = peer(p)
        to(stat_got.at[me], stat_got.at[me], stat_ssem.at[t], stat_rsem.at[me], (g, t)).start()
        to(rows_got.at[me], rows_got.at[me], rows_ssem.at[t], rows_rsem.at[me], (g, t)).start()

    @pl.loop(1, ntp)
    def _(p):
        s = peer(p)
        to(stat_got.at[s], stat_got.at[s], stat_ssem.at[s], stat_rsem.at[s], (g, s)).wait_recv()
        to(rows_got.at[s], rows_got.at[s], rows_ssem.at[s], rows_rsem.at[s], (g, s)).wait_recv()

    stats = stat_got[...].reshape(128, 128).T[0:tokens]
    mean = jnp.sum(jnp.where(lane % 8 == 0, stats, 0.0), axis=1, keepdims=True) * (1.0 / D)
    spread = jnp.sum(jnp.where(lane % 8 == 1, stats, 0.0), axis=1, keepdims=True) * (1.0 / D)
    scale = lax.rsqrt(spread - mean * mean + EPSILON)
    for s in range(ntp):
        shift = stats[:, 8 * s + 2 : 8 * s + 3] - mean
        gains = jnp.concatenate([stat_got[s, 4:5, :], stat_got[s, 5:6, :]], axis=1)
        normed[:, s * width : (s + 1) * width] = (
            (rows_got[s].astype(F32) + shift) * scale * gains
        ).astype(BF16)

    halves = (pl.ds(0, tokens // 2), pl.ds(tokens // 2, tokens // 2))

    def line(half, k, at, some=slice(None)):
        if half == 0:
            return draft_got.at[some, at, k, halves[0]]
        return draft_got.at[at, some, k, halves[1]]

    def pairs(k, base, moves):
        made = []
        for j, (sent, got, where) in enumerate(moves):
            sems = draft_ssem.at[k, base + j], draft_rsem.at[k, base + j]
            made.append(
                (functools.partial(to, sent, sent, *sems, where), functools.partial(to, got, got, *sems, where))
            )
        return made

    def place(half, along, across):
        a, b = lax.rem((mx, mz)[half] + along, side), lax.rem((mx, mz)[1 - half] + across, side)
        return (a, b) if half == 0 else (b, a)

    def first_phase(k):
        moves = []
        for by in (1, side - 1, 2):
            for half in range(2):
                own = draft_got.at[mx, mz, k, halves[half]]
                x, z = place(half, side - by, 0)
                moves.append((own, draft_got.at[x, z, k, halves[half]], hop(half, by)))
        return pairs(k, 0, moves)

    def second_phase(k):
        moves = []
        for by in (1, side - 1):
            for half in range(2):
                mid = (mx, mz)[1 - half]
                got = line(half, k, lax.rem(mid + side - by, side))
                moves.append((line(half, k, mid), got, hop(1 - half, by)))
        return pairs(k, 6, moves)

    def third_phase(k):
        moves = []
        for by, some in ((1, pl.ds(0, side // 2)), (side - 1, pl.ds(side // 2, side // 2))):
            for half in range(2):
                mid = (mx, mz)[1 - half]
                sent = line(half, k, lax.rem(mid + side - by, side), some)
                got = line(half, k, lax.rem(mid + 2, side), some)
                moves.append((sent, got, hop(1 - half, by)))
        return pairs(k, 10, moves)

    def follow(arrived, onward):
        for _, copy in arrived:
            copy().wait_recv()
        for copy, _ in onward:
            copy().start()

    load_d.wait()
    own_rows = normed[:, cols(me)].astype(F32)
    for k in range(DRAFTS):
        update = dot(normed[...], dw[k])
        draft_got[mx, mz, k] = (own_rows + update / (1.0 + jnp.exp(-update))).astype(BF16)
        for copy, _ in first_phase(k):
            copy().start()

    load_w.wait()
    step = 256
    whole = vocab // step

    tiles = [(i * step, step) for i in range(whole)]
    if vocab > whole * step:
        tiles.append((whole * step, vocab - whole * step))

    def base_logits(i):
        at, n = tiles[i]
        logits[0:tokens, at : at + n] = dot_nt(normed[...], vw[at : at + n, :])

    events = [(first_phase(k), second_phase(k)) for k in range(DRAFTS)]
    events += [(second_phase(k), third_phase(k)) for k in range(DRAFTS)]
    for i in range(max(len(tiles), len(events))):
        if i < len(tiles):
            base_logits(i)
        if i < len(events):
            follow(*events[i])

    square[...] = jnp.zeros_like(square)
    square[0:4, 0:tokens] = targets[...].astype(F32)
    wanted = square[...].T[0:tokens]

    for k in range(DRAFTS):
        follow(third_phase(k), ())

    def draft_logits(at, n):
        total = jnp.zeros((DRAFTS * tokens, n), F32)
        for t in range(ntp):
            rows = draft_got[t // side, t % side].reshape(DRAFTS * tokens, width)
            total += dot_nt(rows, vw[pl.ds(at, n), t * width : (t + 1) * width])
        logits[tokens : (DRAFTS + 1) * tokens, pl.ds(at, n)] = total

    @pl.loop(0, whole)
    def _(i):
        draft_logits(pl.multiple_of(i * step, step), step)

    if vocab > whole * step:
        draft_logits(whole * step, vocab - whole * step)

    entry = (lax.broadcasted_iota(jnp.int32, (1, vocab), 1) + me * vocab).astype(F32)
    summary = jnp.zeros((tokens, 128), F32)
    for k in range(DRAFTS + 1):
        x = logits[k * tokens : (k + 1) * tokens, :]
        top = jnp.max(x, axis=1, keepdims=True)
        total = jnp.sum(jnp.exp(x - top), axis=1, keepdims=True)
        picked = jnp.sum(jnp.where(entry == wanted[:, k : k + 1], x, 0.0), axis=1, keepdims=True)
        for c, value in enumerate((top, total, picked)):
            summary = jnp.where(lane == 8 * c + k, value, summary)
    square[0:tokens, :] = summary
    fin_got[me] = square[...].T[0:24]

    @pl.loop(1, ntp)
    def _(p):
        t = peer(p)
        to(fin_got.at[me], fin_got.at[me], fin_ssem.at[t], fin_rsem.at[me], (g, t)).start()

    for k in range(DRAFTS):
        for copy, _ in first_phase(k) + second_phase(k) + third_phase(k):
            copy().wait_send()
    ask.wait_send()
    give_o.wait_send()
    give_s.wait_send()

    @pl.loop(1, ntp)
    def _(p):
        t = peer(p)
        to(rs_send.at[t], rs_got.at[me], rs_ssem.at[t], rs_rsem.at[me], (g, t)).wait_send()
        to(stat_got.at[me], stat_got.at[me], stat_ssem.at[t], stat_rsem.at[me], (g, t)).wait_send()
        to(rows_got.at[me], rows_got.at[me], rows_ssem.at[t], rows_rsem.at[me], (g, t)).wait_send()

    @pl.loop(1, ntp)
    def _(p):
        s = peer(p)
        to(fin_got.at[s], fin_got.at[s], fin_ssem.at[s], fin_rsem.at[s], (g, s)).wait_recv()

    tops, totals, picks = fin_got[:, 0:8, :], fin_got[:, 8:16, :], fin_got[:, 16:24, :]
    top = jnp.max(tops, axis=0)
    total = jnp.sum(totals * jnp.exp(tops - top[None]), axis=0)
    answer = jnp.sum(picks, axis=0) - (top + jnp.log(total))
    probs_out[...] = answer[0:4, 0:tokens]

    @pl.loop(1, ntp)
    def _(p):
        t = peer(p)
        to(fin_got.at[me], fin_got.at[me], fin_ssem.at[t], fin_rsem.at[me], (g, t)).wait_send()


def shards(ntp, *args):
    (
        residual,
        tree_qkv,
        kv_pool,
        page_table,
        cache_len,
        tree_parent,
        accepted_nodes,
        out_weight,
        norm_gain,
        draft_weight,
        vocab_weight,
        target_ids,
    ) = args
    tokens, width = residual.shape
    slots = kv_pool.shape[1]
    side = math.isqrt(ntp)
    used = (2 * HALF + SHORT_PAGES) * PAGE
    vmem = pl.BlockSpec(memory_space=pltpu.VMEM)
    smem = pl.BlockSpec(memory_space=pltpu.SMEM)
    anywhere = pl.BlockSpec(memory_space=pl.ANY)
    dma = pltpu.SemaphoreType.DMA
    return pl.pallas_call(
        functools.partial(kernel, ntp),
        out_shape=(
            jax.ShapeDtypeStruct((DRAFTS + 1, tokens), F32),
            jax.ShapeDtypeStruct((2, 8, width), BF16),
        ),
        in_specs=[vmem, vmem, anywhere, smem, smem, vmem, smem, anywhere, vmem, anywhere, anywhere, vmem],
        out_specs=(vmem, vmem),
        scratch_shapes=[
            pltpu.VMEM((slots, PAGE, width), BF16),
            pltpu.VMEM((slots, PAGE, width), BF16),
            pltpu.VMEM((used, width), BF16),
            pltpu.VMEM((used, width), BF16),
            pltpu.VMEM((width, D), BF16),
            pltpu.VMEM((DRAFTS, D, width), BF16),
            pltpu.VMEM(vocab_weight.shape, BF16),
            pltpu.VMEM((TREE, width), BF16),
            pltpu.VMEM((TREE, width), F32),
            pltpu.VMEM((2 * TREE, 128), F32),
            pltpu.VMEM((TREE, width), F32),
            pltpu.VMEM((2 * TREE, 128), F32),
            pltpu.VMEM((ntp, tokens, width), BF16),
            pltpu.VMEM((ntp, tokens, width), BF16),
            pltpu.VMEM((ntp, tokens, width), BF16),
            pltpu.VMEM((ntp, 8, 128), F32),
            pltpu.VMEM((tokens, D), BF16),
            pltpu.VMEM((side, side, DRAFTS, tokens, width), BF16),
            pltpu.VMEM(((DRAFTS + 1) * tokens, vocab_weight.shape[0]), F32),
            pltpu.VMEM((ntp, 24, 128), F32),
            pltpu.VMEM((128, 128), F32),
            dma((5,)),
            dma((3,)),
            dma((3,)),
            dma((ntp,)),
            dma((ntp,)),
            dma((ntp,)),
            dma((ntp,)),
            dma((ntp,)),
            dma((ntp,)),
            dma((DRAFTS, 14)),
            dma((DRAFTS, 14)),
            dma((ntp,)),
            dma((ntp,)),
        ],
        compiler_params=pltpu.CompilerParams(
            collective_id=0, has_side_effects=True, vmem_limit_bytes=60 * 1024 * 1024
        ),
        cost_estimate=pl.CostEstimate(flops=6_200_000_000, bytes_accessed=27_000_000, transcendentals=1_000_000),
    )(
        residual,
        tree_qkv,
        kv_pool,
        page_table,
        cache_len,
        tree_parent,
        accepted_nodes,
        out_weight,
        norm_gain.reshape(2, width // 2),
        draft_weight,
        vocab_weight,
        target_ids,
    )


def solution(mesh):
    placed = (
        P("group", "tp"),
        P(None, "group", "tp"),
        P(None, "group", None, "tp"),
        P(),
        P(),
        P(),
        P("group", None),
        P("tp", None),
        P("tp"),
        P(None, None, "tp"),
        P("tp", None),
        P(None, "group"),
    )
    return jax.shard_map(
        functools.partial(shards, mesh.shape["tp"]),
        mesh=mesh,
        in_specs=placed,
        out_specs=(P(None, "group"), P(None, "group", "tp")),
        check_vma=False,
    )
```

```python
import functools
import math

import jax
import jax.numpy as jnp
from jax import lax
from jax.experimental import pallas as pl
from jax.experimental.pallas import tpu as pltpu
from jax.sharding import PartitionSpec as P

D = 4096
HEADS = 32
HD = 128
TREE = 48
SHORT_PAGES = 4
HALF = 14
PAGE = 128
DRAFTS = 3
EPSILON = 1e-05
F32 = jnp.float32
BF16 = jnp.bfloat16
MESH = pl.DeviceIdType.MESH
NT = (((1,), (1,)), ((), ()))


def dot(a, b):
    return jnp.dot(a, b, preferred_element_type=F32)


def dot_nt(a, b):
    return lax.dot_general(a, b, NT, preferred_element_type=F32)


def both_heads(rows):
    lane = lax.broadcasted_iota(jnp.int32, rows.shape, 1)
    zero = jnp.zeros_like(rows)
    return jnp.concatenate(
        [jnp.where(lane < HD, rows, zero), jnp.where(lane >= HD, rows, zero)], axis=0
    )


def own_heads(stacked):
    n = stacked.shape[0] // 2
    return jnp.concatenate([stacked[:n, :HD], stacked[n:, HD:]], axis=1)


def wide(column):
    n = column.shape[0] // 2
    return jnp.concatenate(
        [jnp.broadcast_to(column[:n], (n, HD)), jnp.broadcast_to(column[n:], (n, HD))], axis=1
    )


def row_slopes(lane_index, rows):
    second = lax.broadcasted_iota(jnp.int32, (rows, 1), 0) >= rows // 2
    ordinal = (lane_index * 2 + 1 + jnp.where(second, 1, 0)).astype(F32)
    return jnp.exp2(-8.0 * ordinal / HEADS)


def cache_part(queries, keys, values, slopes, length, first, stride):
    span = keys.shape[0]
    scores = dot_nt(queries, keys) * (1.0 / math.sqrt(HD))
    index = lax.broadcasted_iota(jnp.int32, (1, span), 1)
    place = ((index >> 7) * stride + first) * PAGE + (index & (PAGE - 1))
    relative = place.astype(F32) - length
    exists = relative < 0.0
    scores = jnp.where(exists, scores + slopes * relative, -1e30)
    top = jnp.max(scores, axis=1, keepdims=True)
    weights = jnp.where(exists, jnp.exp(scores - top), 0.0)
    total = jnp.sum(weights, axis=1, keepdims=True)
    return top, total, own_heads(dot(weights.astype(BF16), values))


def join(one, two):
    top = jnp.maximum(one[0], two[0])
    f1, f2 = jnp.exp(one[0] - top), jnp.exp(two[0] - top)
    return top, one[1] * f1 + two[1] * f2, one[2] * wide(f1) + two[2] * wide(f2)


def kernel(
    ntp,
    residual,
    tree,
    pool,
    pages,
    lens,
    parents,
    accepted,
    out_w,
    gain,
    draft_w,
    vocab_w,
    targets,
    probs_out,
    kept_out,
    kbank,
    vbank,
    kbuf,
    vbuf,
    ow,
    dw,
    vw,
    guest_q,
    part_o,
    part_s,
    back_o,
    back_s,
    rs_send,
    rs_got,
    rows_got,
    stat_got,
    normed,
    draft_got,
    logits,
    fin_got,
    square,
    hbm_sem,
    pair_send,
    pair_recv,
    rs_ssem,
    rs_rsem,
    rows_ssem,
    rows_rsem,
    stat_ssem,
    stat_rsem,
    draft_ssem,
    draft_rsem,
    fin_ssem,
    fin_rsem,
):
    g = lax.axis_index("group")
    me = lax.axis_index("tp")
    partner = g + 1 - 2 * lax.rem(g, 2)
    tokens, width = residual.shape
    vocab = vw.shape[0]

    def peer(p):
        return lax.rem(me + p, ntp)

    def cols(t):
        return pl.ds(pl.multiple_of(t * width, width), width)

    side = math.isqrt(ntp)
    mx, mz = me // side, lax.rem(me, side)

    def hop(axis, by):
        if axis == 0:
            return (g, lax.rem(mx + by, side) * side + mz)
        return (g, mx * side + lax.rem(mz + by, side))

    def to(src, dst, ssem, rsem, where):
        return pltpu.make_async_remote_copy(
            src_ref=src, dst_ref=dst, send_sem=ssem, recv_sem=rsem, device_id=where, device_id_type=MESH
        )

    def load(src, dst, k):
        return pltpu.make_async_copy(src, dst, hbm_sem.at[k])

    load_k = load(pool.at[0], kbank, 0)
    load_v = load(pool.at[1], vbank, 1)
    load_o = load(out_w, ow, 2)
    load_d = load(draft_w, dw, 3)
    load_w = load(vocab_w, vw, 4)
    load_k.start()
    load_v.start()

    barrier = pltpu.get_barrier_semaphore()
    pl.semaphore_signal(barrier, inc=1, device_id=(partner, me), device_id_type=MESH)

    @pl.loop(1, ntp)
    def _(p):
        pl.semaphore_signal(barrier, inc=1, device_id=(g, peer(p)), device_id_type=MESH)

    parent = jnp.concatenate([parents[pl.ds(2 * g, 1), :], parents[pl.ds(2 * g + 1, 1), :]], axis=1)
    sub = lax.broadcasted_iota(jnp.int32, (tokens, tokens), 0)
    lan = lax.broadcasted_iota(jnp.int32, (tokens, tokens), 1)
    base = jnp.where(lan >= TREE, TREE, 0)
    linked = (parent + base == sub) & (lan != base)
    up = jnp.where(linked | (sub == lan), 1.0, 0.0).astype(BF16)
    for _ in range(TREE.bit_length()):
        up = jnp.minimum(dot(up, up), 1.0).astype(BF16)
    up32 = up.astype(F32)
    depth = jnp.sum(up32, axis=0, keepdims=True) - 1.0
    square[...] = jnp.zeros_like(square)
    square[0:tokens, 0:tokens] = up32
    ancestor = square[...].T[0:tokens, 0:tokens]

    row = lax.broadcasted_iota(jnp.int32, (16, tokens), 0)
    col = lax.broadcasted_iota(jnp.int32, (16, tokens), 1)
    pick = jnp.zeros((16, tokens), jnp.bool_)
    for i in range(8):
        pick = pick | ((row == i) & (col == (i // 4) * TREE + accepted[i // 4, i % 4]))
    chosen = jnp.where(pick, 1.0, 0.0).astype(BF16)
    for c in range(2):
        kept_out[c] = dot(chosen, tree[c + 1])[0:8].astype(BF16)

    pl.semaphore_wait(barrier, ntp)
    ask = to(tree.at[0, pl.ds(TREE, TREE)], guest_q, pair_send.at[0], pair_recv.at[0], (partner, me))
    ask.start()

    slopes = row_slopes(me, 2 * TREE)
    mine, guest = 2 * g + 1, 2 * partner + 1

    load_k.wait()
    load_o.start()
    load_d.start()

    def collect(bank, buf):
        for start, count, request, first, stride in (
            (0, HALF, guest, 1, 2),
            (HALF, HALF, mine, 0, 2),
            (2 * HALF, SHORT_PAGES, 2 * g, 0, 1),
        ):

            @pl.loop(0, count)
            def _(i):
                buf[pl.ds(pl.multiple_of((start + i) * PAGE, PAGE), PAGE), :] = bank[
                    pages[request, first + stride * i]
                ]

    collect(kbank, kbuf)
    load_v.wait()
    load_w.start()
    collect(vbank, vbuf)

    def over(first, count):
        return pl.ds(first * PAGE, count * PAGE)

    short_part = cache_part(
        both_heads(tree[0, 0:TREE]),
        kbuf[over(2 * HALF, SHORT_PAGES)],
        vbuf[over(2 * HALF, SHORT_PAGES)],
        slopes,
        lens[2 * g].astype(F32),
        0,
        1,
    )

    seen = jnp.concatenate([ancestor, ancestor], axis=0) > 0.5
    scores = dot_nt(both_heads(tree[0]), tree[1]) * (1.0 / math.sqrt(HD))
    scores = jnp.where(seen, scores + row_slopes(me, 2 * tokens) * depth, -1e30)
    top = jnp.max(scores, axis=1, keepdims=True)
    weights = jnp.where(seen, jnp.exp(scores - top), 0.0)
    total = jnp.sum(weights, axis=1, keepdims=True)
    out = own_heads(dot(weights.astype(BF16), tree[2]))

    def of_request(r):
        at = r * TREE
        return (
            jnp.concatenate([top[at : at + TREE], top[tokens + at : tokens + at + TREE]], 0),
            jnp.concatenate([total[at : at + TREE], total[tokens + at : tokens + at + TREE]], 0),
            out[at : at + TREE],
        )

    def project(h, merged):
        attn = (merged[2] / wide(merged[1])).astype(BF16)
        for t in range(ntp):
            rs_send[h, t] = dot(attn, ow[:, t * width : (t + 1) * width]).astype(BF16)

        @pl.loop(1, ntp)
        def _(p):
            t = peer(p)
            to(rs_send.at[h, t], rs_got.at[h, me], rs_ssem.at[h, t], rs_rsem.at[h, me], (g, t)).start()

    load_o.wait()
    project(0, join(of_request(0), short_part))
    long = of_request(1)

    ask.wait_recv()
    top, total, out = cache_part(
        both_heads(guest_q[...]),
        kbuf[over(0, HALF)],
        vbuf[over(0, HALF)],
        slopes,
        lens[guest].astype(F32),
        1,
        2,
    )
    part_o[...] = out
    lane = lax.broadcasted_iota(jnp.int32, (2 * TREE, 128), 1)
    part_s[...] = jnp.where(lane < 64, top, total)
    give_o = to(part_o, back_o, pair_send.at[1], pair_recv.at[1], (partner, me))
    give_s = to(part_s, back_s, pair_send.at[2], pair_recv.at[2], (partner, me))
    give_o.start()
    give_s.start()

    long_part = cache_part(
        both_heads(tree[0, TREE : 2 * TREE]),
        kbuf[over(HALF, HALF)],
        vbuf[over(HALF, HALF)],
        slopes,
        lens[mine].astype(F32),
        0,
        2,
    )
    long = join(long, long_part)
    give_o.wait_recv()
    give_s.wait_recv()
    back = back_s[...]
    project(1, join(long, (back[:, 0:1], back[:, 64:65], back_o[...])))

    lane = lax.broadcasted_iota(jnp.int32, (TREE, 128), 1)

    def share_rows(h):
        def add_share(p, so_far):
            s = peer(p)
            to(rs_send.at[h, s], rs_got.at[h, s], rs_ssem.at[h, s], rs_rsem.at[h, s], (g, s)).wait_recv()
            return so_far + rs_got[h, s].astype(F32)

        hidden = residual[h * TREE : (h + 1) * TREE, :].astype(F32) + rs_send[h, me].astype(F32)
        hidden = lax.fori_loop(1, ntp, add_share, hidden)
        block_sum = jnp.sum(hidden, axis=1, keepdims=True)
        block_square = jnp.sum(hidden * hidden, axis=1, keepdims=True)
        block_mean = block_sum * (1.0 / width)
        rows_got[h, me] = (hidden - block_mean).astype(BF16)
        square[0:TREE, :] = jnp.where(
            lane == 0, block_sum, jnp.where(lane == 1, block_square, jnp.where(lane == 2, block_mean, 0.0))
        )
        stat_got[h, me] = square[...].T[0:8]
        stat_got[h, me, 4:6, :] = gain[...]

        @pl.loop(1, ntp)
        def _(p):
            t = peer(p)
            stat, rows = stat_got.at[h, me], rows_got.at[h, me]
            to(stat, stat, stat_ssem.at[h, t], stat_rsem.at[h, me], (g, t)).start()
            to(rows, rows, rows_ssem.at[h, t], rows_rsem.at[h, me], (g, t)).start()

    def normalise(h):
        @pl.loop(1, ntp)
        def _(p):
            s = peer(p)
            stat, rows = stat_got.at[h, s], rows_got.at[h, s]
            to(stat, stat, stat_ssem.at[h, s], stat_rsem.at[h, s], (g, s)).wait_recv()
            to(rows, rows, rows_ssem.at[h, s], rows_rsem.at[h, s], (g, s)).wait_recv()

        stats = stat_got[h].reshape(128, 128).T[0:TREE]
        mean = jnp.sum(jnp.where(lane % 8 == 0, stats, 0.0), axis=1, keepdims=True) * (1.0 / D)
        spread = jnp.sum(jnp.where(lane % 8 == 1, stats, 0.0), axis=1, keepdims=True) * (1.0 / D)
        scale = lax.rsqrt(spread - mean * mean + EPSILON)
        for s in range(ntp):
            shift = stats[:, 8 * s + 2 : 8 * s + 3] - mean
            gains = jnp.concatenate([stat_got[h, s, 4:5, :], stat_got[h, s, 5:6, :]], axis=1)
            normed[h * TREE : (h + 1) * TREE, s * width : (s + 1) * width] = (
                (rows_got[h, s].astype(F32) + shift) * scale * gains
            ).astype(BF16)

    def line(half, k, at, some=slice(None)):
        rows = pl.ds(half * TREE, TREE)
        return draft_got.at[some, at, k, rows] if half == 0 else draft_got.at[at, some, k, rows]

    def pairs(half, k, base, moves):
        made = []
        for j, (sent, got, where) in enumerate(moves):
            sems = draft_ssem.at[half, k, base + j], draft_rsem.at[half, k, base + j]
            made.append(
                (functools.partial(to, sent, sent, *sems, where), functools.partial(to, got, got, *sems, where))
            )
        return made

    def first_phase(half, k):
        moves = []
        rows = pl.ds(half * TREE, TREE)
        for by in (1, side - 1, 2):
            from_there = lax.rem((mx, mz)[half] + side - by, side)
            x, z = (from_there, mz) if half == 0 else (mx, from_there)
            moves.append((draft_got.at[mx, mz, k, rows], draft_got.at[x, z, k, rows], hop(half, by)))
        return pairs(half, k, 0, moves)

    def second_phase(half, k):
        moves = []
        mid = (mx, mz)[1 - half]
        for by in (1, side - 1):
            got = line(half, k, lax.rem(mid + side - by, side))
            moves.append((line(half, k, mid), got, hop(1 - half, by)))
        return pairs(half, k, 3, moves)

    def third_phase(half, k):
        moves = []
        mid = (mx, mz)[1 - half]
        for by, some in ((1, pl.ds(0, side // 2)), (side - 1, pl.ds(side // 2, side // 2))):
            sent = line(half, k, lax.rem(mid + side - by, side), some)
            got = line(half, k, lax.rem(mid + 2, side), some)
            moves.append((sent, got, hop(1 - half, by)))
        return pairs(half, k, 5, moves)

    def follow(arrived, onward):
        for _, copy in arrived:
            copy().wait_recv()
        for copy, _ in onward:
            copy().start()

    def one_two(half, k):
        follow(first_phase(half, k), second_phase(half, k))

    def two_three(half, k):
        follow(second_phase(half, k), third_phase(half, k))

    def draft(h, k):
        rows = slice(h * TREE, (h + 1) * TREE)
        update = dot(normed[rows, :], dw[k])
        own_rows = normed[rows, cols(me)].astype(F32)
        draft_got[mx, mz, k, rows, :] = (own_rows + update / (1.0 + jnp.exp(-update))).astype(BF16)
        follow((), first_phase(h, k))

    share_rows(0)
    share_rows(1)
    normalise(0)
    load_d.wait()
    for k in range(DRAFTS):
        draft(0, k)
    one_two(0, 0)
    one_two(0, 1)
    normalise(1)
    draft(1, 0)
    one_two(0, 2)
    draft(1, 1)
    two_three(0, 0)
    draft(1, 2)

    load_w.wait()
    step = 256
    whole = vocab // step

    tiles = [(i * step, step) for i in range(whole)]
    if vocab > whole * step:
        tiles.append((whole * step, vocab - whole * step))

    def base_logits(i):
        at, n = tiles[i]
        logits[0:tokens, at : at + n] = dot_nt(normed[...], vw[at : at + n, :])

    events = (
        (one_two, 1, 0),
        (two_three, 0, 1),
        (one_two, 1, 1),
        (two_three, 0, 2),
        (one_two, 1, 2),
        (two_three, 1, 0),
        (two_three, 1, 1),
        (two_three, 1, 2),
    )
    for i in range(max(len(tiles), len(events))):
        if i < len(tiles):
            base_logits(i)
        if i < len(events):
            event, half, k = events[i]
            event(half, k)

    square[...] = jnp.zeros_like(square)
    square[0:4, 0:tokens] = targets[...].astype(F32)
    wanted = square[...].T[0:tokens]

    for k in range(DRAFTS):
        for half in range(2):
            follow(third_phase(half, k), ())

    def draft_logits(at, n):
        total = jnp.zeros((DRAFTS * tokens, n), F32)
        for t in range(ntp):
            rows = draft_got[t // side, t % side].reshape(DRAFTS * tokens, width)
            total += dot_nt(rows, vw[pl.ds(at, n), t * width : (t + 1) * width])
        logits[tokens : (DRAFTS + 1) * tokens, pl.ds(at, n)] = total

    @pl.loop(0, whole)
    def _(i):
        draft_logits(pl.multiple_of(i * step, step), step)

    if vocab > whole * step:
        draft_logits(whole * step, vocab - whole * step)

    entry = (lax.broadcasted_iota(jnp.int32, (1, vocab), 1) + me * vocab).astype(F32)
    summary = jnp.zeros((tokens, 128), F32)
    lane = lax.broadcasted_iota(jnp.int32, (tokens, 128), 1)
    for k in range(DRAFTS + 1):
        x = logits[k * tokens : (k + 1) * tokens, :]
        top = jnp.max(x, axis=1, keepdims=True)
        total = jnp.sum(jnp.exp(x - top), axis=1, keepdims=True)
        picked = jnp.sum(jnp.where(entry == wanted[:, k : k + 1], x, 0.0), axis=1, keepdims=True)
        for c, value in enumerate((top, total, picked)):
            summary = jnp.where(lane == 8 * c + k, value, summary)
    square[0:tokens, :] = summary
    fin_got[me] = square[...].T[0:24]

    @pl.loop(1, ntp)
    def _(p):
        t = peer(p)
        to(fin_got.at[me], fin_got.at[me], fin_ssem.at[t], fin_rsem.at[me], (g, t)).start()

    for k in range(DRAFTS):
        for half in range(2):
            for copy, _ in first_phase(half, k) + second_phase(half, k) + third_phase(half, k):
                copy().wait_send()
    ask.wait_send()
    give_o.wait_send()
    give_s.wait_send()

    @pl.loop(1, ntp)
    def _(p):
        t = peer(p)
        for h in range(2):
            stat, rows = stat_got.at[h, me], rows_got.at[h, me]
            to(rs_send.at[h, t], rs_got.at[h, me], rs_ssem.at[h, t], rs_rsem.at[h, me], (g, t)).wait_send()
            to(stat, stat, stat_ssem.at[h, t], stat_rsem.at[h, me], (g, t)).wait_send()
            to(rows, rows, rows_ssem.at[h, t], rows_rsem.at[h, me], (g, t)).wait_send()

    @pl.loop(1, ntp)
    def _(p):
        s = peer(p)
        to(fin_got.at[s], fin_got.at[s], fin_ssem.at[s], fin_rsem.at[s], (g, s)).wait_recv()

    tops, totals, picks = fin_got[:, 0:8, :], fin_got[:, 8:16, :], fin_got[:, 16:24, :]
    top = jnp.max(tops, axis=0)
    total = jnp.sum(totals * jnp.exp(tops - top[None]), axis=0)
    answer = jnp.sum(picks, axis=0) - (top + jnp.log(total))
    probs_out[...] = answer[0:4, 0:tokens]

    @pl.loop(1, ntp)
    def _(p):
        t = peer(p)
        to(fin_got.at[me], fin_got.at[me], fin_ssem.at[t], fin_rsem.at[me], (g, t)).wait_send()


def shards(ntp, *args):
    (
        residual,
        tree_qkv,
        kv_pool,
        page_table,
        cache_len,
        tree_parent,
        accepted_nodes,
        out_weight,
        norm_gain,
        draft_weight,
        vocab_weight,
        target_ids,
    ) = args
    tokens, width = residual.shape
    slots = kv_pool.shape[1]
    side = math.isqrt(ntp)
    used = (2 * HALF + SHORT_PAGES) * PAGE
    vmem = pl.BlockSpec(memory_space=pltpu.VMEM)
    smem = pl.BlockSpec(memory_space=pltpu.SMEM)
    anywhere = pl.BlockSpec(memory_space=pl.ANY)
    dma = pltpu.SemaphoreType.DMA
    return pl.pallas_call(
        functools.partial(kernel, ntp),
        out_shape=(
            jax.ShapeDtypeStruct((DRAFTS + 1, tokens), F32),
            jax.ShapeDtypeStruct((2, 8, width), BF16),
        ),
        in_specs=[vmem, vmem, anywhere, smem, smem, vmem, smem, anywhere, vmem, anywhere, anywhere, vmem],
        out_specs=(vmem, vmem),
        scratch_shapes=[
            pltpu.VMEM((slots, PAGE, width), BF16),
            pltpu.VMEM((slots, PAGE, width), BF16),
            pltpu.VMEM((used, width), BF16),
            pltpu.VMEM((used, width), BF16),
            pltpu.VMEM((width, D), BF16),
            pltpu.VMEM((DRAFTS, D, width), BF16),
            pltpu.VMEM(vocab_weight.shape, BF16),
            pltpu.VMEM((TREE, width), BF16),
            pltpu.VMEM((TREE, width), F32),
            pltpu.VMEM((2 * TREE, 128), F32),
            pltpu.VMEM((TREE, width), F32),
            pltpu.VMEM((2 * TREE, 128), F32),
            pltpu.VMEM((2, ntp, TREE, width), BF16),
            pltpu.VMEM((2, ntp, TREE, width), BF16),
            pltpu.VMEM((2, ntp, TREE, width), BF16),
            pltpu.VMEM((2, ntp, 8, 128), F32),
            pltpu.VMEM((tokens, D), BF16),
            pltpu.VMEM((side, side, DRAFTS, tokens, width), BF16),
            pltpu.VMEM(((DRAFTS + 1) * tokens, vocab_weight.shape[0]), F32),
            pltpu.VMEM((ntp, 24, 128), F32),
            pltpu.VMEM((128, 128), F32),
            dma((5,)),
            dma((3,)),
            dma((3,)),
            dma((2, ntp)),
            dma((2, ntp)),
            dma((2, ntp)),
            dma((2, ntp)),
            dma((2, ntp)),
            dma((2, ntp)),
            dma((2, DRAFTS, 7)),
            dma((2, DRAFTS, 7)),
            dma((ntp,)),
            dma((ntp,)),
        ],
        compiler_params=pltpu.CompilerParams(
            collective_id=0, has_side_effects=True, vmem_limit_bytes=60 * 1024 * 1024
        ),
        cost_estimate=pl.CostEstimate(flops=6_200_000_000, bytes_accessed=27_000_000, transcendentals=1_000_000),
    )(
        residual,
        tree_qkv,
        kv_pool,
        page_table,
        cache_len,
        tree_parent,
        accepted_nodes,
        out_weight,
        norm_gain.reshape(2, width // 2),
        draft_weight,
        vocab_weight,
        target_ids,
    )


def solution(mesh):
    placed = (
        P("group", "tp"),
        P(None, "group", "tp"),
        P(None, "group", None, "tp"),
        P(),
        P(),
        P(),
        P("group", None),
        P("tp", None),
        P("tp"),
        P(None, None, "tp"),
        P("tp", None),
        P(None, "group"),
    )
    return jax.shard_map(
        functools.partial(shards, mesh.shape["tp"]),
        mesh=mesh,
        in_specs=placed,
        out_specs=(P(None, "group"), P(None, "group", "tp")),
        check_vma=False,
    )
```

```python
import functools
import math

import jax
import jax.numpy as jnp
from jax import lax
from jax.experimental import pallas as pl
from jax.experimental.pallas import tpu as pltpu
from jax.sharding import PartitionSpec as P

D = 4096
HEADS = 32
HD = 128
TREE = 48
SHORT_PAGES = 4
HALF = 14
PAGE = 128
DRAFTS = 3
EPSILON = 1e-05
F32 = jnp.float32
BF16 = jnp.bfloat16
MESH = pl.DeviceIdType.MESH
NT = (((1,), (1,)), ((), ()))


def dot(a, b):
    return jnp.dot(a, b, preferred_element_type=F32)


def dot_nt(a, b):
    return lax.dot_general(a, b, NT, preferred_element_type=F32)


def both_heads(rows):
    lane = lax.broadcasted_iota(jnp.int32, rows.shape, 1)
    zero = jnp.zeros_like(rows)
    return jnp.concatenate(
        [jnp.where(lane < HD, rows, zero), jnp.where(lane >= HD, rows, zero)], axis=0
    )


def own_heads(stacked):
    n = stacked.shape[0] // 2
    return jnp.concatenate([stacked[:n, :HD], stacked[n:, HD:]], axis=1)


def wide(column):
    n = column.shape[0] // 2
    return jnp.concatenate(
        [jnp.broadcast_to(column[:n], (n, HD)), jnp.broadcast_to(column[n:], (n, HD))], axis=1
    )


def row_slopes(lane_index, rows):
    second = lax.broadcasted_iota(jnp.int32, (rows, 1), 0) >= rows // 2
    ordinal = (lane_index * 2 + 1 + jnp.where(second, 1, 0)).astype(F32)
    return jnp.exp2(-8.0 * ordinal / HEADS)


def cache_part(queries, keys, values, slopes, length, first, stride):
    span = keys.shape[0]
    scores = dot_nt(queries, keys) * (1.0 / math.sqrt(HD))
    index = lax.broadcasted_iota(jnp.int32, (1, span), 1)
    place = ((index >> 7) * stride + first) * PAGE + (index & (PAGE - 1))
    relative = place.astype(F32) - length
    exists = relative < 0.0
    scores = jnp.where(exists, scores + slopes * relative, -1e30)
    top = jnp.max(scores, axis=1, keepdims=True)
    weights = jnp.where(exists, jnp.exp(scores - top), 0.0)
    total = jnp.sum(weights, axis=1, keepdims=True)
    return top, total, own_heads(dot(weights.astype(BF16), values))


def join(one, two):
    top = jnp.maximum(one[0], two[0])
    f1, f2 = jnp.exp(one[0] - top), jnp.exp(two[0] - top)
    return top, one[1] * f1 + two[1] * f2, one[2] * wide(f1) + two[2] * wide(f2)


def kernel(
    ntp,
    residual,
    tree,
    pool,
    pages,
    lens,
    parents,
    accepted,
    out_w,
    gain,
    draft_w,
    vocab_w,
    targets,
    probs_out,
    kept_out,
    kbank,
    vbank,
    kbuf,
    vbuf,
    ow,
    dw,
    vw,
    guest_q,
    part_o,
    part_s,
    back_o,
    back_s,
    rs_send,
    rs_got,
    stat_got,
    normed,
    spread,
    logits,
    fin_got,
    square,
    hbm_sem,
    pair_send,
    pair_recv,
    rs_ssem,
    rs_rsem,
    stat_ssem,
    stat_rsem,
    ring_ssem,
    ring_rsem,
    fin_ssem,
    fin_rsem,
):
    g = lax.axis_index("group")
    me = lax.axis_index("tp")
    partner = g + 1 - 2 * lax.rem(g, 2)
    tokens, width = residual.shape
    vocab = vw.shape[0]

    def peer(p):
        return lax.rem(me + p, ntp)

    def cols(t):
        return pl.ds(pl.multiple_of(t * width, width), width)

    side = math.isqrt(ntp)
    mx, mz = me // side, lax.rem(me, side)

    def hop(axis, by):
        if axis == 0:
            return (g, lax.rem(mx + by, side) * side + mz)
        return (g, mx * side + lax.rem(mz + by, side))

    def to(src, dst, ssem, rsem, where):
        return pltpu.make_async_remote_copy(
            src_ref=src, dst_ref=dst, send_sem=ssem, recv_sem=rsem, device_id=where, device_id_type=MESH
        )

    def load(src, dst, k):
        return pltpu.make_async_copy(src, dst, hbm_sem.at[k])

    load_k = load(pool.at[0], kbank, 0)
    load_v = load(pool.at[1], vbank, 1)
    load_o = load(out_w, ow, 2)
    load_d = load(draft_w, dw, 3)
    load_w = load(vocab_w, vw, 4)
    load_k.start()
    load_v.start()

    barrier = pltpu.get_barrier_semaphore()
    pl.semaphore_signal(barrier, inc=1, device_id=(partner, me), device_id_type=MESH)

    @pl.loop(1, ntp)
    def _(p):
        pl.semaphore_signal(barrier, inc=1, device_id=(g, peer(p)), device_id_type=MESH)

    parent = jnp.concatenate([parents[pl.ds(2 * g, 1), :], parents[pl.ds(2 * g + 1, 1), :]], axis=1)
    sub = lax.broadcasted_iota(jnp.int32, (tokens, tokens), 0)
    lan = lax.broadcasted_iota(jnp.int32, (tokens, tokens), 1)
    base = jnp.where(lan >= TREE, TREE, 0)
    linked = (parent + base == sub) & (lan != base)
    up = jnp.where(linked | (sub == lan), 1.0, 0.0).astype(BF16)
    for _ in range(TREE.bit_length()):
        up = jnp.minimum(dot(up, up), 1.0).astype(BF16)
    up32 = up.astype(F32)
    depth = jnp.sum(up32, axis=0, keepdims=True) - 1.0
    square[...] = jnp.zeros_like(square)
    square[0:tokens, 0:tokens] = up32
    ancestor = square[...].T[0:tokens, 0:tokens]

    row = lax.broadcasted_iota(jnp.int32, (16, tokens), 0)
    col = lax.broadcasted_iota(jnp.int32, (16, tokens), 1)
    pick = jnp.zeros((16, tokens), jnp.bool_)
    for i in range(8):
        pick = pick | ((row == i) & (col == (i // 4) * TREE + accepted[i // 4, i % 4]))
    chosen = jnp.where(pick, 1.0, 0.0).astype(BF16)
    for c in range(2):
        kept_out[c] = dot(chosen, tree[c + 1])[0:8].astype(BF16)

    pl.semaphore_wait(barrier, ntp)
    ask = to(tree.at[0, pl.ds(TREE, TREE)], guest_q, pair_send.at[0], pair_recv.at[0], (partner, me))
    ask.start()

    slopes = row_slopes(me, 2 * TREE)
    mine, guest = 2 * g + 1, 2 * partner + 1

    load_k.wait()
    load_o.start()
    load_d.start()

    def collect(bank, buf):
        for start, count, request, first, stride in (
            (0, HALF, guest, 1, 2),
            (HALF, HALF, mine, 0, 2),
            (2 * HALF, SHORT_PAGES, 2 * g, 0, 1),
        ):

            @pl.loop(0, count)
            def _(i):
                buf[pl.ds(pl.multiple_of((start + i) * PAGE, PAGE), PAGE), :] = bank[
                    pages[request, first + stride * i]
                ]

    collect(kbank, kbuf)
    load_v.wait()
    load_w.start()
    collect(vbank, vbuf)

    def over(first, count):
        return pl.ds(first * PAGE, count * PAGE)

    short_part = cache_part(
        both_heads(tree[0, 0:TREE]),
        kbuf[over(2 * HALF, SHORT_PAGES)],
        vbuf[over(2 * HALF, SHORT_PAGES)],
        slopes,
        lens[2 * g].astype(F32),
        0,
        1,
    )

    seen = jnp.concatenate([ancestor, ancestor], axis=0) > 0.5
    scores = dot_nt(both_heads(tree[0]), tree[1]) * (1.0 / math.sqrt(HD))
    scores = jnp.where(seen, scores + row_slopes(me, 2 * tokens) * depth, -1e30)
    top = jnp.max(scores, axis=1, keepdims=True)
    weights = jnp.where(seen, jnp.exp(scores - top), 0.0)
    total = jnp.sum(weights, axis=1, keepdims=True)
    out = own_heads(dot(weights.astype(BF16), tree[2]))

    def of_request(r):
        at = r * TREE
        return (
            jnp.concatenate([top[at : at + TREE], top[tokens + at : tokens + at + TREE]], 0),
            jnp.concatenate([total[at : at + TREE], total[tokens + at : tokens + at + TREE]], 0),
            out[at : at + TREE],
        )

    def project(h, merged):
        attn = (merged[2] / wide(merged[1])).astype(BF16)
        for t in range(ntp):
            rs_send[h, t] = dot(attn, ow[:, t * width : (t + 1) * width]).astype(BF16)

        @pl.loop(1, ntp)
        def _(p):
            t = peer(p)
            to(rs_send.at[h, t], rs_got.at[h, me], rs_ssem.at[h, t], rs_rsem.at[h, me], (g, t)).start()

    load_o.wait()
    project(0, join(of_request(0), short_part))
    long = of_request(1)

    ask.wait_recv()
    top, total, out = cache_part(
        both_heads(guest_q[...]),
        kbuf[over(0, HALF)],
        vbuf[over(0, HALF)],
        slopes,
        lens[guest].astype(F32),
        1,
        2,
    )
    part_o[...] = out
    lane = lax.broadcasted_iota(jnp.int32, (2 * TREE, 128), 1)
    part_s[...] = jnp.where(lane < 64, top, total)
    give_o = to(part_o, back_o, pair_send.at[1], pair_recv.at[1], (partner, me))
    give_s = to(part_s, back_s, pair_send.at[2], pair_recv.at[2], (partner, me))
    give_o.start()
    give_s.start()

    long_part = cache_part(
        both_heads(tree[0, TREE : 2 * TREE]),
        kbuf[over(HALF, HALF)],
        vbuf[over(HALF, HALF)],
        slopes,
        lens[mine].astype(F32),
        0,
        2,
    )
    long = join(long, long_part)
    give_o.wait_recv()
    give_s.wait_recv()
    back = back_s[...]
    project(1, join(long, (back[:, 0:1], back[:, 64:65], back_o[...])))

    half_width = width // 2
    here = (mx, mz)

    def line(item, half, at, some=slice(None)):
        return spread.at[item, half, some, at] if half == 0 else spread.at[item, half, at, some]

    def moves(item, half, base, made):
        out = []
        for j, (sent, got, where) in enumerate(made):
            sems = ring_ssem.at[item, half, base + j], ring_rsem.at[item, half, base + j]
            out.append(
                (functools.partial(to, sent, sent, *sems, where), functools.partial(to, got, got, *sems, where))
            )
        return out

    def first_phase(item):
        out = []
        for half in range(2):
            made = []
            for by in (1, side - 1, 2):
                other = lax.rem(here[half] + side - by, side)
                x, z = (other, mz) if half == 0 else (mx, other)
                made.append((spread.at[item, half, mx, mz], spread.at[item, half, x, z], hop(half, by)))
            out += moves(item, half, 0, made)
        return out

    def second_phase(item):
        out = []
        for half in range(2):
            mid = here[1 - half]
            made = []
            for by in (1, side - 1) + ((2,) if item < 2 else ()):
                got = line(item, half, lax.rem(mid + side - by, side))
                made.append((line(item, half, mid), got, hop(1 - half, by)))
            out += moves(item, half, 3, made)
        return out

    def third_phase(item):
        out = []
        for half in range(2):
            mid = here[1 - half]
            made = []
            for by, some in ((1, pl.ds(0, side // 2)), (side - 1, pl.ds(side // 2, side // 2))):
                sent = line(item, half, lax.rem(mid + side - by, side), some)
                got = line(item, half, lax.rem(mid + 2, side), some)
                made.append((sent, got, hop(1 - half, by)))
            out += moves(item, half, 5, made)
        return out

    def follow(arrived, onward):
        for _, copy in arrived:
            copy().wait_recv()
        for copy, _ in onward:
            copy().start()

    def one_two(item):
        follow(first_phase(item), second_phase(item))

    def two_three(item):
        follow(second_phase(item), third_phase(item))

    def publish(item, rows):
        rows = rows.astype(BF16)
        for half in range(2):
            spread[item, half, mx, mz] = rows[:, half * half_width : (half + 1) * half_width]
        follow((), first_phase(item))

    lane = lax.broadcasted_iota(jnp.int32, (TREE, 128), 1)

    def share_rows(h):
        def add_share(p, so_far):
            s = peer(p)
            to(rs_send.at[h, s], rs_got.at[h, s], rs_ssem.at[h, s], rs_rsem.at[h, s], (g, s)).wait_recv()
            return so_far + rs_got[h, s].astype(F32)

        hidden = residual[h * TREE : (h + 1) * TREE, :].astype(F32) + rs_send[h, me].astype(F32)
        hidden = lax.fori_loop(1, ntp, add_share, hidden)
        block_sum = jnp.sum(hidden, axis=1, keepdims=True)
        block_square = jnp.sum(hidden * hidden, axis=1, keepdims=True)
        block_mean = block_sum * (1.0 / width)
        square[0:TREE, :] = jnp.where(
            lane == 0, block_sum, jnp.where(lane == 1, block_square, jnp.where(lane == 2, block_mean, 0.0))
        )
        stat_got[h, me] = square[...].T[0:8]
        stat_got[h, me, 4:6, :] = gain[...]

        @pl.loop(1, ntp)
        def _(p):
            t = peer(p)
            stat = stat_got.at[h, me]
            to(stat, stat, stat_ssem.at[h, t], stat_rsem.at[h, me], (g, t)).start()

        publish(h, hidden - block_mean)

    def normalise(h):
        @pl.loop(1, ntp)
        def _(p):
            s = peer(p)
            stat = stat_got.at[h, s]
            to(stat, stat, stat_ssem.at[h, s], stat_rsem.at[h, s], (g, s)).wait_recv()

        follow(second_phase(h), ())

        stats = stat_got[h].reshape(128, 128).T[0:TREE]
        mean = jnp.sum(jnp.where(lane % 8 == 0, stats, 0.0), axis=1, keepdims=True) * (1.0 / D)
        squares = jnp.sum(jnp.where(lane % 8 == 1, stats, 0.0), axis=1, keepdims=True) * (1.0 / D)
        scale = lax.rsqrt(squares - mean * mean + EPSILON)
        for s in range(ntp):
            shift = stats[:, 8 * s + 2 : 8 * s + 3] - mean
            gains = jnp.concatenate([stat_got[h, s, 4:5, :], stat_got[h, s, 5:6, :]], axis=1)
            rows = jnp.concatenate([spread[h, half, s // side, s % side] for half in range(2)], axis=1)
            normed[h * TREE : (h + 1) * TREE, s * width : (s + 1) * width] = (
                (rows.astype(F32) + shift) * scale * gains
            ).astype(BF16)

    def draft(h, k):
        rows = slice(h * TREE, (h + 1) * TREE)
        update = dot(normed[rows, :], dw[k])
        own_rows = normed[rows, cols(me)].astype(F32)
        publish(2 + 2 * k + h, own_rows + update / (1.0 + jnp.exp(-update)))

    def item(h, k):
        return 2 + 2 * k + h

    share_rows(0)
    one_two(0)
    share_rows(1)
    normalise(0)
    load_d.wait()
    draft(0, 0)
    one_two(1)
    draft(0, 1)
    draft(0, 2)
    one_two(item(0, 0))
    normalise(1)
    draft(1, 0)
    one_two(item(0, 1))
    draft(1, 1)
    one_two(item(0, 2))
    two_three(item(0, 0))
    draft(1, 2)
    one_two(item(1, 0))
    two_three(item(0, 1))

    load_w.wait()
    step = 256
    whole = vocab // step

    tiles = [(i * step, step) for i in range(whole)]
    if vocab > whole * step:
        tiles.append((whole * step, vocab - whole * step))

    def base_logits(i):
        at, n = tiles[i]
        logits[0:tokens, at : at + n] = dot_nt(normed[...], vw[at : at + n, :])

    events = (
        ((one_two, 1, 1), (two_three, 0, 2)),
        ((one_two, 1, 2),),
        ((two_three, 1, 0),),
        (),
        ((two_three, 1, 1),),
        (),
        ((two_three, 1, 2),),
    )
    for i in range(max(len(tiles), len(events))):
        if i < len(tiles):
            base_logits(i)
        if i < len(events):
            for event, h, k in events[i]:
                event(item(h, k))

    square[...] = jnp.zeros_like(square)
    square[0:4, 0:tokens] = targets[...].astype(F32)
    wanted = square[...].T[0:tokens]

    drafts = DRAFTS * tokens

    def some_drafts(at, n, lines):
        total = jnp.zeros((drafts, n), F32)
        for half in range(2):
            for by in lines:
                mid = lax.rem(here[1 - half] + by, side)
                for first in range(0, side, 2):
                    rows, weights = [], []
                    for other in (first, first + 1):
                        x, z = (other, mid) if half == 0 else (mid, other)
                        rows.append(spread[2 : 2 * (DRAFTS + 1), half, x, z].reshape(drafts, half_width))
                        place = (x * side + z) * width + half * half_width
                        weights.append(vw[pl.ds(at, n), pl.ds(pl.multiple_of(place, half_width), half_width)])
                    total += dot_nt(jnp.concatenate(rows, axis=1), jnp.concatenate(weights, axis=1))
        return total

    def each_tile(body):
        @pl.loop(0, whole)
        def _(i):
            body(pl.multiple_of(i * step, step), step)

        if vocab > whole * step:
            body(whole * step, vocab - whole * step)

    def near(at, n):
        logits[tokens : tokens + drafts, pl.ds(at, n)] = some_drafts(at, n, (0, 1, side - 1))

    def far(at, n):
        logits[tokens : tokens + drafts, pl.ds(at, n)] += some_drafts(at, n, (2,))

    each_tile(near)
    for k in range(DRAFTS):
        for h in range(2):
            follow(third_phase(item(h, k)), ())
    each_tile(far)

    entry = (lax.broadcasted_iota(jnp.int32, (1, vocab), 1) + me * vocab).astype(F32)
    summary = jnp.zeros((tokens, 128), F32)
    lane = lax.broadcasted_iota(jnp.int32, (tokens, 128), 1)
    for k in range(DRAFTS + 1):
        x = logits[k * tokens : (k + 1) * tokens, :]
        top = jnp.max(x, axis=1, keepdims=True)
        total = jnp.sum(jnp.exp(x - top), axis=1, keepdims=True)
        picked = jnp.sum(jnp.where(entry == wanted[:, k : k + 1], x, 0.0), axis=1, keepdims=True)
        for c, value in enumerate((top, total, picked)):
            summary = jnp.where(lane == 8 * c + k, value, summary)
    square[0:tokens, :] = summary
    fin_got[me] = square[...].T[0:24]

    @pl.loop(1, ntp)
    def _(p):
        t = peer(p)
        to(fin_got.at[me], fin_got.at[me], fin_ssem.at[t], fin_rsem.at[me], (g, t)).start()

    for i in range(2 * (DRAFTS + 1)):
        for copy, _ in first_phase(i) + second_phase(i) + (third_phase(i) if i >= 2 else []):
            copy().wait_send()
    ask.wait_send()
    give_o.wait_send()
    give_s.wait_send()

    @pl.loop(1, ntp)
    def _(p):
        t = peer(p)
        for h in range(2):
            stat = stat_got.at[h, me]
            to(rs_send.at[h, t], rs_got.at[h, me], rs_ssem.at[h, t], rs_rsem.at[h, me], (g, t)).wait_send()
            to(stat, stat, stat_ssem.at[h, t], stat_rsem.at[h, me], (g, t)).wait_send()

    @pl.loop(1, ntp)
    def _(p):
        s = peer(p)
        to(fin_got.at[s], fin_got.at[s], fin_ssem.at[s], fin_rsem.at[s], (g, s)).wait_recv()

    tops, totals, picks = fin_got[:, 0:8, :], fin_got[:, 8:16, :], fin_got[:, 16:24, :]
    top = jnp.max(tops, axis=0)
    total = jnp.sum(totals * jnp.exp(tops - top[None]), axis=0)
    answer = jnp.sum(picks, axis=0) - (top + jnp.log(total))
    probs_out[...] = answer[0:4, 0:tokens]

    @pl.loop(1, ntp)
    def _(p):
        t = peer(p)
        to(fin_got.at[me], fin_got.at[me], fin_ssem.at[t], fin_rsem.at[me], (g, t)).wait_send()


def shards(ntp, *args):
    (
        residual,
        tree_qkv,
        kv_pool,
        page_table,
        cache_len,
        tree_parent,
        accepted_nodes,
        out_weight,
        norm_gain,
        draft_weight,
        vocab_weight,
        target_ids,
    ) = args
    tokens, width = residual.shape
    slots = kv_pool.shape[1]
    side = math.isqrt(ntp)
    used = (2 * HALF + SHORT_PAGES) * PAGE
    vmem = pl.BlockSpec(memory_space=pltpu.VMEM)
    smem = pl.BlockSpec(memory_space=pltpu.SMEM)
    anywhere = pl.BlockSpec(memory_space=pl.ANY)
    dma = pltpu.SemaphoreType.DMA
    return pl.pallas_call(
        functools.partial(kernel, ntp),
        out_shape=(
            jax.ShapeDtypeStruct((DRAFTS + 1, tokens), F32),
            jax.ShapeDtypeStruct((2, 8, width), BF16),
        ),
        in_specs=[vmem, vmem, anywhere, smem, smem, vmem, smem, anywhere, vmem, anywhere, anywhere, vmem],
        out_specs=(vmem, vmem),
        scratch_shapes=[
            pltpu.VMEM((slots, PAGE, width), BF16),
            pltpu.VMEM((slots, PAGE, width), BF16),
            pltpu.VMEM((used, width), BF16),
            pltpu.VMEM((used, width), BF16),
            pltpu.VMEM((width, D), BF16),
            pltpu.VMEM((DRAFTS, D, width), BF16),
            pltpu.VMEM(vocab_weight.shape, BF16),
            pltpu.VMEM((TREE, width), BF16),
            pltpu.VMEM((TREE, width), F32),
            pltpu.VMEM((2 * TREE, 128), F32),
            pltpu.VMEM((TREE, width), F32),
            pltpu.VMEM((2 * TREE, 128), F32),
            pltpu.VMEM((2, ntp, TREE, width), BF16),
            pltpu.VMEM((2, ntp, TREE, width), BF16),
            pltpu.VMEM((2, ntp, 8, 128), F32),
            pltpu.VMEM((tokens, D), BF16),
            pltpu.VMEM((2 * (DRAFTS + 1), 2, side, side, TREE, width // 2), BF16),
            pltpu.VMEM(((DRAFTS + 1) * tokens, vocab_weight.shape[0]), F32),
            pltpu.VMEM((ntp, 24, 128), F32),
            pltpu.VMEM((128, 128), F32),
            dma((5,)),
            dma((3,)),
            dma((3,)),
            dma((2, ntp)),
            dma((2, ntp)),
            dma((2, ntp)),
            dma((2, ntp)),
            dma((2 * (DRAFTS + 1), 2, 7)),
            dma((2 * (DRAFTS + 1), 2, 7)),
            dma((ntp,)),
            dma((ntp,)),
        ],
        compiler_params=pltpu.CompilerParams(
            collective_id=0, has_side_effects=True, vmem_limit_bytes=60 * 1024 * 1024
        ),
        cost_estimate=pl.CostEstimate(flops=6_200_000_000, bytes_accessed=27_000_000, transcendentals=1_000_000),
    )(
        residual,
        tree_qkv,
        kv_pool,
        page_table,
        cache_len,
        tree_parent,
        accepted_nodes,
        out_weight,
        norm_gain.reshape(2, width // 2),
        draft_weight,
        vocab_weight,
        target_ids,
    )


def solution(mesh):
    placed = (
        P("group", "tp"),
        P(None, "group", "tp"),
        P(None, "group", None, "tp"),
        P(),
        P(),
        P(),
        P("group", None),
        P("tp", None),
        P("tp"),
        P(None, None, "tp"),
        P("tp", None),
        P(None, "group"),
    )
    return jax.shard_map(
        functools.partial(shards, mesh.shape["tp"]),
        mesh=mesh,
        in_specs=placed,
        out_specs=(P(None, "group"), P(None, "group", "tp")),
        check_vma=False,
    )
```

```python
import functools
import math

import jax
import jax.numpy as jnp
from jax import lax
from jax.experimental import pallas as pl
from jax.experimental.pallas import tpu as pltpu
from jax.sharding import PartitionSpec as P

D = 4096
HEADS = 32
HD = 128
TREE = 48
SHORT_PAGES = 4
HALF = 14
PAGE = 128
DRAFTS = 3
EPSILON = 1e-05
ROUTED = (0, 1, 3, 5, 7)
F32 = jnp.float32
BF16 = jnp.bfloat16
MESH = pl.DeviceIdType.MESH
NT = (((1,), (1,)), ((), ()))


def dot(a, b):
    return jnp.dot(a, b, preferred_element_type=F32)


def dot_nt(a, b):
    return lax.dot_general(a, b, NT, preferred_element_type=F32)


def both_heads(rows):
    lane = lax.broadcasted_iota(jnp.int32, rows.shape, 1)
    zero = jnp.zeros_like(rows)
    return jnp.concatenate(
        [jnp.where(lane < HD, rows, zero), jnp.where(lane >= HD, rows, zero)], axis=0
    )


def own_heads(stacked):
    n = stacked.shape[0] // 2
    return jnp.concatenate([stacked[:n, :HD], stacked[n:, HD:]], axis=1)


def wide(column):
    n = column.shape[0] // 2
    return jnp.concatenate(
        [jnp.broadcast_to(column[:n], (n, HD)), jnp.broadcast_to(column[n:], (n, HD))], axis=1
    )


def row_slopes(lane_index, rows):
    second = lax.broadcasted_iota(jnp.int32, (rows, 1), 0) >= rows // 2
    ordinal = (lane_index * 2 + 1 + jnp.where(second, 1, 0)).astype(F32)
    return jnp.exp2(-8.0 * ordinal / HEADS)


def cache_part(queries, keys, values, slopes, length, first, stride):
    span = keys.shape[0]
    scores = dot_nt(queries, keys) * (1.0 / math.sqrt(HD))
    index = lax.broadcasted_iota(jnp.int32, (1, span), 1)
    place = ((index >> 7) * stride + first) * PAGE + (index & (PAGE - 1))
    relative = place.astype(F32) - length
    exists = relative < 0.0
    scores = jnp.where(exists, scores + slopes * relative, -1e30)
    top = jnp.max(scores, axis=1, keepdims=True)
    weights = jnp.where(exists, jnp.exp(scores - top), 0.0)
    total = jnp.sum(weights, axis=1, keepdims=True)
    return top, total, own_heads(dot(weights.astype(BF16), values))


def join(one, two):
    top = jnp.maximum(one[0], two[0])
    f1, f2 = jnp.exp(one[0] - top), jnp.exp(two[0] - top)
    return top, one[1] * f1 + two[1] * f2, one[2] * wide(f1) + two[2] * wide(f2)


def kernel(
    ntp,
    residual,
    tree,
    pool,
    pages,
    lens,
    parents,
    accepted,
    out_w,
    gain,
    draft_w,
    vocab_w,
    targets,
    probs_out,
    kept_out,
    kbank,
    vbank,
    kbuf,
    vbuf,
    ow,
    dw,
    vw,
    guest_q,
    part_o,
    part_s,
    back_o,
    back_s,
    rs_send,
    rs_got,
    stat_got,
    acts,
    spread,
    logits,
    fin_got,
    square,
    hbm_sem,
    pair_send,
    pair_recv,
    rs_ssem,
    rs_rsem,
    stat_ssem,
    stat_rsem,
    ring_ssem,
    ring_rsem,
    fin_ssem,
    fin_rsem,
):
    g = lax.axis_index("group")
    me = lax.axis_index("tp")
    partner = g + 1 - 2 * lax.rem(g, 2)
    tokens, width = residual.shape
    vocab = vw.shape[0]

    def peer(p):
        return lax.rem(me + p, ntp)

    def cols(t):
        return pl.ds(pl.multiple_of(t * width, width), width)

    side = math.isqrt(ntp)
    mx, mz = me // side, lax.rem(me, side)

    def hop(axis, by):
        if axis == 0:
            return (g, lax.rem(mx + by, side) * side + mz)
        return (g, mx * side + lax.rem(mz + by, side))

    def to(src, dst, ssem, rsem, where):
        return pltpu.make_async_remote_copy(
            src_ref=src, dst_ref=dst, send_sem=ssem, recv_sem=rsem, device_id=where, device_id_type=MESH
        )

    def load(src, dst, k):
        return pltpu.make_async_copy(src, dst, hbm_sem.at[k])

    load_k = load(pool.at[0], kbank, 0)
    load_v = load(pool.at[1], vbank, 1)
    load_o = load(out_w, ow, 2)
    load_d = load(draft_w, dw, 3)
    load_w = load(vocab_w, vw, 4)
    for copy in (load_k, load_v, load_o, load_d, load_w):
        copy.start()

    barrier = pltpu.get_barrier_semaphore()
    pl.semaphore_signal(barrier, inc=1, device_id=(partner, me), device_id_type=MESH)

    @pl.loop(1, ntp)
    def _(p):
        pl.semaphore_signal(barrier, inc=1, device_id=(g, peer(p)), device_id_type=MESH)

    parent = jnp.concatenate([parents[pl.ds(2 * g, 1), :], parents[pl.ds(2 * g + 1, 1), :]], axis=1)
    sub = lax.broadcasted_iota(jnp.int32, (tokens, tokens), 0)
    lan = lax.broadcasted_iota(jnp.int32, (tokens, tokens), 1)
    base = jnp.where(lan >= TREE, TREE, 0)
    linked = (parent + base == sub) & (lan != base)
    up = jnp.where(linked | (sub == lan), 1.0, 0.0).astype(BF16)
    for _ in range(TREE.bit_length()):
        up = jnp.minimum(dot(up, up), 1.0).astype(BF16)
    up32 = up.astype(F32)
    depth = jnp.sum(up32, axis=0, keepdims=True) - 1.0
    square[...] = jnp.zeros_like(square)
    square[0:tokens, 0:tokens] = up32
    ancestor = square[...].T[0:tokens, 0:tokens]

    row = lax.broadcasted_iota(jnp.int32, (16, tokens), 0)
    col = lax.broadcasted_iota(jnp.int32, (16, tokens), 1)
    pick = jnp.zeros((16, tokens), jnp.bool_)
    for i in range(8):
        pick = pick | ((row == i) & (col == (i // 4) * TREE + accepted[i // 4, i % 4]))
    chosen = jnp.where(pick, 1.0, 0.0).astype(BF16)
    for c in range(2):
        kept_out[c] = dot(chosen, tree[c + 1])[0:8].astype(BF16)

    pl.semaphore_wait(barrier, ntp)
    ask = to(tree.at[0, pl.ds(TREE, TREE)], guest_q, pair_send.at[0], pair_recv.at[0], (partner, me))
    ask.start()

    slopes = row_slopes(me, 2 * TREE)
    mine, guest = 2 * g + 1, 2 * partner + 1

    load_k.wait()

    def collect(bank, buf):
        for start, count, request, first, stride in (
            (0, HALF, guest, 1, 2),
            (HALF, HALF, mine, 0, 2),
            (2 * HALF, SHORT_PAGES, 2 * g, 0, 1),
        ):

            for i in range(count):
                buf[(start + i) * PAGE : (start + i + 1) * PAGE, :] = bank[pages[request, first + stride * i]]

    collect(kbank, kbuf)
    load_v.wait()
    collect(vbank, vbuf)

    def over(first, count):
        return pl.ds(first * PAGE, count * PAGE)

    short_part = cache_part(
        both_heads(tree[0, 0:TREE]),
        kbuf[over(2 * HALF, SHORT_PAGES)],
        vbuf[over(2 * HALF, SHORT_PAGES)],
        slopes,
        lens[2 * g].astype(F32),
        0,
        1,
    )

    seen = jnp.concatenate([ancestor, ancestor], axis=0) > 0.5
    scores = dot_nt(both_heads(tree[0]), tree[1]) * (1.0 / math.sqrt(HD))
    scores = jnp.where(seen, scores + row_slopes(me, 2 * tokens) * depth, -1e30)
    top = jnp.max(scores, axis=1, keepdims=True)
    weights = jnp.where(seen, jnp.exp(scores - top), 0.0)
    total = jnp.sum(weights, axis=1, keepdims=True)
    out = own_heads(dot(weights.astype(BF16), tree[2]))

    def of_request(r):
        at = r * TREE
        return (
            jnp.concatenate([top[at : at + TREE], top[tokens + at : tokens + at + TREE]], 0),
            jnp.concatenate([total[at : at + TREE], total[tokens + at : tokens + at + TREE]], 0),
            out[at : at + TREE],
        )

    def project(h, merged):
        attn = (merged[2] / wide(merged[1])).astype(BF16)
        for t in range(ntp):
            rs_send[h, t] = dot(attn, ow[:, t * width : (t + 1) * width]).astype(BF16)

        @pl.loop(1, ntp)
        def _(p):
            t = peer(p)
            to(rs_send.at[h, t], rs_got.at[h, me], rs_ssem.at[h, t], rs_rsem.at[h, me], (g, t)).start()

    load_o.wait()
    project(0, join(of_request(0), short_part))
    long = of_request(1)

    ask.wait_recv()
    top, total, out = cache_part(
        both_heads(guest_q[...]),
        kbuf[over(0, HALF)],
        vbuf[over(0, HALF)],
        slopes,
        lens[guest].astype(F32),
        1,
        2,
    )
    part_o[...] = out
    lane = lax.broadcasted_iota(jnp.int32, (2 * TREE, 128), 1)
    part_s[...] = jnp.where(lane < 64, top, total)
    give_o = to(part_o, back_o, pair_send.at[1], pair_recv.at[1], (partner, me))
    give_s = to(part_s, back_s, pair_send.at[2], pair_recv.at[2], (partner, me))
    give_o.start()
    give_s.start()

    long_part = cache_part(
        both_heads(tree[0, TREE : 2 * TREE]),
        kbuf[over(HALF, HALF)],
        vbuf[over(HALF, HALF)],
        slopes,
        lens[mine].astype(F32),
        0,
        2,
    )
    long = join(long, long_part)
    give_o.wait_recv()
    give_s.wait_recv()
    back = back_s[...]
    project(1, join(long, (back[:, 0:1], back[:, 64:65], back_o[...])))

    half_width = width // 2
    here = (mx, mz)

    def line(item, half, at, some=slice(None)):
        return spread.at[item, half, some, at] if half == 0 else spread.at[item, half, at, some]

    def moves(item, half, base, made):
        out = []
        for j, (sent, got, where) in enumerate(made):
            sems = ring_ssem.at[item, half, base + j], ring_rsem.at[item, half, base + j]
            out.append(
                (functools.partial(to, sent, sent, *sems, where), functools.partial(to, got, got, *sems, where))
            )
        return out

    def first_phase(item):
        out = []
        for half in range(2):
            made = []
            for by in (1, side - 1, 2):
                other = lax.rem(here[half] + side - by, side)
                x, z = (other, mz) if half == 0 else (mx, other)
                made.append((spread.at[item, half, mx, mz], spread.at[item, half, x, z], hop(half, by)))
            out += moves(item, half, 0, made)
        return out

    def second_phase(item):
        out = []
        for half in range(2):
            mid = here[1 - half]
            made = []
            for by in (1, side - 1):
                got = line(item, half, lax.rem(mid + side - by, side))
                made.append((line(item, half, mid), got, hop(1 - half, by)))
            out += moves(item, half, 3, made)
        return out

    def last_phase(item):
        out = []
        for half in range(2):
            mid = here[1 - half]
            opposite = lax.rem(mid + 2, side)
            made = []
            if item in ROUTED:
                made.append((line(item, half, mid), line(item, half, opposite), hop(1 - half, 2)))
            else:
                for by, some in ((1, pl.ds(0, side // 2)), (side - 1, pl.ds(side // 2, side // 2))):
                    sent = line(item, half, lax.rem(mid + side - by, side), some)
                    made.append((sent, line(item, half, opposite, some), hop(1 - half, by)))
            out += moves(item, half, 5, made)
        return out

    def follow(arrived, onward):
        for _, copy in arrived:
            copy().wait_recv()
        for copy, _ in onward:
            copy().start()

    def one_two(item):
        follow(first_phase(item), second_phase(item) + (last_phase(item) if item in ROUTED else []))

    def two_three(item):
        follow(second_phase(item), [] if item in ROUTED else last_phase(item))

    def publish(item, rows):
        rows = rows.astype(BF16)
        for half in range(2):
            spread[item, half, mx, mz] = rows[:, half * half_width : (half + 1) * half_width]
        follow((), first_phase(item))

    lane = lax.broadcasted_iota(jnp.int32, (TREE, 128), 1)

    def share_rows(h):
        def add_share(p, so_far):
            s = peer(p)
            to(rs_send.at[h, s], rs_got.at[h, s], rs_ssem.at[h, s], rs_rsem.at[h, s], (g, s)).wait_recv()
            return so_far + rs_got[h, s].astype(F32)

        hidden = residual[h * TREE : (h + 1) * TREE, :].astype(F32) + rs_send[h, me].astype(F32)
        hidden = lax.fori_loop(1, ntp, add_share, hidden)
        block_sum = jnp.sum(hidden, axis=1, keepdims=True)
        block_square = jnp.sum(hidden * hidden, axis=1, keepdims=True)
        block_mean = block_sum * (1.0 / width)
        square[0:TREE, :] = jnp.where(
            lane == 0, block_sum, jnp.where(lane == 1, block_square, jnp.where(lane == 2, block_mean, 0.0))
        )
        stat_got[h, me] = square[...].T[0:8]
        stat_got[h, me, 4:6, :] = gain[...]

        @pl.loop(1, ntp)
        def _(p):
            t = peer(p)
            stat = stat_got.at[h, me]
            to(stat, stat, stat_ssem.at[h, t], stat_rsem.at[h, me], (g, t)).start()

        publish(h, hidden - block_mean)

    group = (DRAFTS + 1) * TREE

    def normalise(h):
        @pl.loop(1, ntp)
        def _(p):
            s = peer(p)
            stat = stat_got.at[h, s]
            to(stat, stat, stat_ssem.at[h, s], stat_rsem.at[h, s], (g, s)).wait_recv()

        follow(second_phase(h) + last_phase(h), ())

        stats = stat_got[h].reshape(128, 128).T[0:TREE]
        mean = jnp.sum(jnp.where(lane % 8 == 0, stats, 0.0), axis=1, keepdims=True) * (1.0 / D)
        squares = jnp.sum(jnp.where(lane % 8 == 1, stats, 0.0), axis=1, keepdims=True) * (1.0 / D)
        scale = lax.rsqrt(squares - mean * mean + EPSILON)
        for s in range(ntp):
            shift = stats[:, 8 * s + 2 : 8 * s + 3] - mean
            gains = jnp.concatenate([stat_got[h, s, 4:5, :], stat_got[h, s, 5:6, :]], axis=1)
            rows = jnp.concatenate([spread[h, half, s // side, s % side] for half in range(2)], axis=1)
            acts[h * group : h * group + TREE, s * width : (s + 1) * width] = (
                (rows.astype(F32) + shift) * scale * gains
            ).astype(BF16)

    def draft(h, k):
        rows = slice(h * group, h * group + TREE)
        update = dot(acts[rows, :], dw[k])
        own_rows = acts[rows, cols(me)].astype(F32)
        publish(2 + 2 * k + h, own_rows + update / (1.0 + jnp.exp(-update)))

    def item(h, k):
        return 2 + 2 * k + h

    share_rows(0)
    one_two(0)
    share_rows(1)
    one_two(1)
    normalise(0)
    load_d.wait()
    for k in range(DRAFTS):
        draft(0, k)
    one_two(item(0, 0))
    normalise(1)
    draft(1, 0)
    one_two(item(0, 1))
    draft(1, 1)
    draft(1, 2)
    one_two(item(0, 2))
    two_three(item(0, 0))

    square[...] = jnp.zeros_like(square)
    square[0:4, 0:tokens] = targets[...].astype(F32)
    wanted = square[...].T[0:tokens]

    one_two(item(1, 0))
    two_three(item(0, 1))
    one_two(item(1, 1))
    two_three(item(0, 2))
    one_two(item(1, 2))

    load_w.wait()
    step = 256
    whole = vocab // step
    entry = (lax.broadcasted_iota(jnp.int32, (1, vocab), 1) + me * vocab).astype(F32)

    def vocabulary(h):
        for k in range(DRAFTS):
            if item(h, k) in ROUTED:
                follow(second_phase(item(h, k)), ())
            follow(last_phase(item(h, k)), ())
            at = h * group + (k + 1) * TREE
            for s in range(ntp):
                acts[at : at + TREE, s * width : (s + 1) * width] = jnp.concatenate(
                    [spread[item(h, k), half, s // side, s % side] for half in range(2)], axis=1
                )

        def block(at, n):
            logits[h * group : (h + 1) * group, pl.ds(at, n)] = dot_nt(
                acts[h * group : (h + 1) * group, :], vw[pl.ds(at, n), :]
            )

        @pl.loop(0, whole)
        def _(i):
            block(pl.multiple_of(i * step, step), step)

        if vocab > whole * step:
            block(whole * step, vocab - whole * step)

        summary = jnp.zeros((TREE, 128), F32)
        for k in range(DRAFTS + 1):
            x = logits[h * group + k * TREE : h * group + (k + 1) * TREE, :]
            top = jnp.max(x, axis=1, keepdims=True)
            total = jnp.sum(jnp.exp(x - top), axis=1, keepdims=True)
            target = wanted[h * TREE : (h + 1) * TREE, k : k + 1]
            picked = jnp.sum(jnp.where(entry == target, x, 0.0), axis=1, keepdims=True)
            for c, value in enumerate((top, total, picked)):
                summary = jnp.where(lane == 8 * c + k, value, summary)
        square[h * TREE : (h + 1) * TREE, :] = summary

    vocabulary(0)
    vocabulary(1)
    fin_got[me] = square[...].T[0:24]

    @pl.loop(1, ntp)
    def _(p):
        t = peer(p)
        to(fin_got.at[me], fin_got.at[me], fin_ssem.at[t], fin_rsem.at[me], (g, t)).start()

    for i in range(2 * (DRAFTS + 1)):
        for copy, _ in first_phase(i) + second_phase(i) + last_phase(i):
            copy().wait_send()
    ask.wait_send()
    give_o.wait_send()
    give_s.wait_send()

    @pl.loop(1, ntp)
    def _(p):
        t = peer(p)
        for h in range(2):
            stat = stat_got.at[h, me]
            to(rs_send.at[h, t], rs_got.at[h, me], rs_ssem.at[h, t], rs_rsem.at[h, me], (g, t)).wait_send()
            to(stat, stat, stat_ssem.at[h, t], stat_rsem.at[h, me], (g, t)).wait_send()

    @pl.loop(1, ntp)
    def _(p):
        s = peer(p)
        to(fin_got.at[s], fin_got.at[s], fin_ssem.at[s], fin_rsem.at[s], (g, s)).wait_recv()

    tops, totals, picks = fin_got[:, 0:8, :], fin_got[:, 8:16, :], fin_got[:, 16:24, :]
    top = jnp.max(tops, axis=0)
    total = jnp.sum(totals * jnp.exp(tops - top[None]), axis=0)
    answer = jnp.sum(picks, axis=0) - (top + jnp.log(total))
    probs_out[...] = answer[0:4, 0:tokens]

    @pl.loop(1, ntp)
    def _(p):
        t = peer(p)
        to(fin_got.at[me], fin_got.at[me], fin_ssem.at[t], fin_rsem.at[me], (g, t)).wait_send()


def shards(ntp, *args):
    (
        residual,
        tree_qkv,
        kv_pool,
        page_table,
        cache_len,
        tree_parent,
        accepted_nodes,
        out_weight,
        norm_gain,
        draft_weight,
        vocab_weight,
        target_ids,
    ) = args
    tokens, width = residual.shape
    slots = kv_pool.shape[1]
    side = math.isqrt(ntp)
    used = (2 * HALF + SHORT_PAGES) * PAGE
    vmem = pl.BlockSpec(memory_space=pltpu.VMEM)
    smem = pl.BlockSpec(memory_space=pltpu.SMEM)
    anywhere = pl.BlockSpec(memory_space=pl.ANY)
    dma = pltpu.SemaphoreType.DMA
    return pl.pallas_call(
        functools.partial(kernel, ntp),
        out_shape=(
            jax.ShapeDtypeStruct((DRAFTS + 1, tokens), F32),
            jax.ShapeDtypeStruct((2, 8, width), BF16),
        ),
        in_specs=[vmem, vmem, anywhere, smem, smem, vmem, smem, anywhere, vmem, anywhere, anywhere, vmem],
        out_specs=(vmem, vmem),
        scratch_shapes=[
            pltpu.VMEM((slots, PAGE, width), BF16),
            pltpu.VMEM((slots, PAGE, width), BF16),
            pltpu.VMEM((used, width), BF16),
            pltpu.VMEM((used, width), BF16),
            pltpu.VMEM((width, D), BF16),
            pltpu.VMEM((DRAFTS, D, width), BF16),
            pltpu.VMEM(vocab_weight.shape, BF16),
            pltpu.VMEM((TREE, width), BF16),
            pltpu.VMEM((TREE, width), F32),
            pltpu.VMEM((2 * TREE, 128), F32),
            pltpu.VMEM((TREE, width), F32),
            pltpu.VMEM((2 * TREE, 128), F32),
            pltpu.VMEM((2, ntp, TREE, width), BF16),
            pltpu.VMEM((2, ntp, TREE, width), BF16),
            pltpu.VMEM((2, ntp, 8, 128), F32),
            pltpu.VMEM(((DRAFTS + 1) * tokens, D), BF16),
            pltpu.VMEM((2 * (DRAFTS + 1), 2, side, side, TREE, width // 2), BF16),
            pltpu.VMEM(((DRAFTS + 1) * tokens, vocab_weight.shape[0]), F32),
            pltpu.VMEM((ntp, 24, 128), F32),
            pltpu.VMEM((128, 128), F32),
            dma((5,)),
            dma((3,)),
            dma((3,)),
            dma((2, ntp)),
            dma((2, ntp)),
            dma((2, ntp)),
            dma((2, ntp)),
            dma((2 * (DRAFTS + 1), 2, 7)),
            dma((2 * (DRAFTS + 1), 2, 7)),
            dma((ntp,)),
            dma((ntp,)),
        ],
        compiler_params=pltpu.CompilerParams(
            collective_id=0, has_side_effects=True, vmem_limit_bytes=60 * 1024 * 1024
        ),
        cost_estimate=pl.CostEstimate(flops=6_200_000_000, bytes_accessed=27_000_000, transcendentals=1_000_000),
    )(
        residual,
        tree_qkv,
        kv_pool,
        page_table,
        cache_len,
        tree_parent,
        accepted_nodes,
        out_weight,
        norm_gain.reshape(2, width // 2),
        draft_weight,
        vocab_weight,
        target_ids,
    )


def solution(mesh):
    placed = (
        P("group", "tp"),
        P(None, "group", "tp"),
        P(None, "group", None, "tp"),
        P(),
        P(),
        P(),
        P("group", None),
        P("tp", None),
        P("tp"),
        P(None, None, "tp"),
        P("tp", None),
        P(None, "group"),
    )
    return jax.shard_map(
        functools.partial(shards, mesh.shape["tp"]),
        mesh=mesh,
        in_specs=placed,
        out_specs=(P(None, "group"), P(None, "group", "tp")),
        check_vma=False,
    )
```

```python
import functools
import math

import jax
import jax.numpy as jnp
from jax import lax
from jax.experimental import pallas as pl
from jax.experimental.pallas import tpu as pltpu
from jax.sharding import PartitionSpec as P

D = 4096
HEADS = 32
HD = 128
TREE = 48
SHORT_PAGES = 4
HALF = 14
PAGE = 128
DRAFTS = 3
EPSILON = 1e-05
STEP = 512
ROUTED = (0, 1, 3, 5, 7)
F32 = jnp.float32
BF16 = jnp.bfloat16
MESH = pl.DeviceIdType.MESH
NT = (((1,), (1,)), ((), ()))


def dot(a, b):
    return jnp.dot(a, b, preferred_element_type=F32)


def dot_nt(a, b):
    return lax.dot_general(a, b, NT, preferred_element_type=F32)


def both_heads(rows):
    lane = lax.broadcasted_iota(jnp.int32, rows.shape, 1)
    zero = jnp.zeros_like(rows)
    return jnp.concatenate(
        [jnp.where(lane < HD, rows, zero), jnp.where(lane >= HD, rows, zero)], axis=0
    )


def own_heads(stacked):
    n = stacked.shape[0] // 2
    return jnp.concatenate([stacked[:n, :HD], stacked[n:, HD:]], axis=1)


def wide(column):
    n = column.shape[0] // 2
    return jnp.concatenate(
        [jnp.broadcast_to(column[:n], (n, HD)), jnp.broadcast_to(column[n:], (n, HD))], axis=1
    )


def row_slopes(lane_index, rows):
    second = lax.broadcasted_iota(jnp.int32, (rows, 1), 0) >= rows // 2
    ordinal = (lane_index * 2 + 1 + jnp.where(second, 1, 0)).astype(F32)
    return jnp.exp2(-8.0 * ordinal / HEADS)


def cache_part(queries, keys, values, slopes, length, first, stride):
    span = keys.shape[0]
    scores = dot_nt(queries, keys) * (1.0 / math.sqrt(HD))
    index = lax.broadcasted_iota(jnp.int32, (1, span), 1)
    place = ((index >> 7) * stride + first) * PAGE + (index & (PAGE - 1))
    relative = place.astype(F32) - length
    exists = relative < 0.0
    scores = jnp.where(exists, scores + slopes * relative, -1e30)
    top = jnp.max(scores, axis=1, keepdims=True)
    weights = jnp.where(exists, jnp.exp(scores - top), 0.0)
    total = jnp.sum(weights, axis=1, keepdims=True)
    return top, total, own_heads(dot(weights.astype(BF16), values))


def join(one, two):
    top = jnp.maximum(one[0], two[0])
    f1, f2 = jnp.exp(one[0] - top), jnp.exp(two[0] - top)
    return top, one[1] * f1 + two[1] * f2, one[2] * wide(f1) + two[2] * wide(f2)


def kernel(
    ntp,
    residual,
    tree,
    pool,
    pages,
    lens,
    parents,
    accepted,
    out_w,
    gain,
    draft_w,
    vocab_w,
    targets,
    probs_out,
    kept_out,
    kbank,
    vbank,
    kbuf,
    vbuf,
    ow,
    dw,
    vw,
    guest_q,
    part_o,
    part_s,
    back_o,
    back_s,
    rs_send,
    rs_got,
    stat_got,
    acts,
    spread,
    logits,
    fin_got,
    square,
    hbm_sem,
    pair_send,
    pair_recv,
    rs_ssem,
    rs_rsem,
    stat_ssem,
    stat_rsem,
    ring_ssem,
    ring_rsem,
    fin_ssem,
    fin_rsem,
):
    g = lax.axis_index("group")
    me = lax.axis_index("tp")
    partner = g + 1 - 2 * lax.rem(g, 2)
    tokens, width = residual.shape
    vocab = vw.shape[0]

    def peer(p):
        return lax.rem(me + p, ntp)

    def cols(t):
        return pl.ds(pl.multiple_of(t * width, width), width)

    side = math.isqrt(ntp)
    mx, mz = me // side, lax.rem(me, side)

    def hop(axis, by):
        if axis == 0:
            return (g, lax.rem(mx + by, side) * side + mz)
        return (g, mx * side + lax.rem(mz + by, side))

    def to(src, dst, ssem, rsem, where):
        return pltpu.make_async_remote_copy(
            src_ref=src, dst_ref=dst, send_sem=ssem, recv_sem=rsem, device_id=where, device_id_type=MESH
        )

    def load(src, dst, k):
        return pltpu.make_async_copy(src, dst, hbm_sem.at[k])

    load_k = load(pool.at[0], kbank, 0)
    load_v = load(pool.at[1], vbank, 1)
    load_o = load(out_w, ow, 2)
    load_d = load(draft_w, dw, 3)
    load_w = load(vocab_w, vw, 4)
    for copy in (load_k, load_v, load_o, load_d, load_w):
        copy.start()

    barrier = pltpu.get_barrier_semaphore()
    pl.semaphore_signal(barrier, inc=1, device_id=(partner, me), device_id_type=MESH)

    @pl.loop(1, ntp)
    def _(p):
        pl.semaphore_signal(barrier, inc=1, device_id=(g, peer(p)), device_id_type=MESH)

    parent = jnp.concatenate([parents[pl.ds(2 * g, 1), :], parents[pl.ds(2 * g + 1, 1), :]], axis=1)
    sub = lax.broadcasted_iota(jnp.int32, (tokens, tokens), 0)
    lan = lax.broadcasted_iota(jnp.int32, (tokens, tokens), 1)
    base = jnp.where(lan >= TREE, TREE, 0)
    linked = (parent + base == sub) & (lan != base)
    up = jnp.where(linked | (sub == lan), 1.0, 0.0).astype(BF16)
    for _ in range(TREE.bit_length()):
        up = jnp.minimum(dot(up, up), 1.0).astype(BF16)
    up32 = up.astype(F32)
    depth = jnp.sum(up32, axis=0, keepdims=True) - 1.0
    square[...] = jnp.zeros_like(square)
    square[0:tokens, 0:tokens] = up32
    ancestor = square[...].T[0:tokens, 0:tokens]

    row = lax.broadcasted_iota(jnp.int32, (16, tokens), 0)
    col = lax.broadcasted_iota(jnp.int32, (16, tokens), 1)
    pick = jnp.zeros((16, tokens), jnp.bool_)
    for i in range(8):
        pick = pick | ((row == i) & (col == (i // 4) * TREE + accepted[i // 4, i % 4]))
    chosen = jnp.where(pick, 1.0, 0.0).astype(BF16)
    for c in range(2):
        kept_out[c] = dot(chosen, tree[c + 1])[0:8].astype(BF16)

    pl.semaphore_wait(barrier, ntp)
    ask = to(tree.at[0, pl.ds(TREE, TREE)], guest_q, pair_send.at[0], pair_recv.at[0], (partner, me))
    ask.start()

    slopes = row_slopes(me, 2 * TREE)
    mine, guest = 2 * g + 1, 2 * partner + 1

    load_k.wait()

    def collect(bank, buf):
        for start, count, request, first, stride in (
            (0, HALF, guest, 1, 2),
            (HALF, HALF, mine, 0, 2),
            (2 * HALF, SHORT_PAGES, 2 * g, 0, 1),
        ):

            for i in range(count):
                buf[(start + i) * PAGE : (start + i + 1) * PAGE, :] = bank[pages[request, first + stride * i]]

    collect(kbank, kbuf)
    load_v.wait()
    collect(vbank, vbuf)

    def over(first, count):
        return pl.ds(first * PAGE, count * PAGE)

    short_part = cache_part(
        both_heads(tree[0, 0:TREE]),
        kbuf[over(2 * HALF, SHORT_PAGES)],
        vbuf[over(2 * HALF, SHORT_PAGES)],
        slopes,
        lens[2 * g].astype(F32),
        0,
        1,
    )

    seen = jnp.concatenate([ancestor, ancestor], axis=0) > 0.5
    scores = dot_nt(both_heads(tree[0]), tree[1]) * (1.0 / math.sqrt(HD))
    scores = jnp.where(seen, scores + row_slopes(me, 2 * tokens) * depth, -1e30)
    top = jnp.max(scores, axis=1, keepdims=True)
    weights = jnp.where(seen, jnp.exp(scores - top), 0.0)
    total = jnp.sum(weights, axis=1, keepdims=True)
    out = own_heads(dot(weights.astype(BF16), tree[2]))

    def of_request(r):
        at = r * TREE
        return (
            jnp.concatenate([top[at : at + TREE], top[tokens + at : tokens + at + TREE]], 0),
            jnp.concatenate([total[at : at + TREE], total[tokens + at : tokens + at + TREE]], 0),
            out[at : at + TREE],
        )

    def project(h, merged):
        attn = (merged[2] / wide(merged[1])).astype(BF16)
        for t in range(ntp):
            rs_send[h, t] = dot(attn, ow[:, t * width : (t + 1) * width]).astype(BF16)

        @pl.loop(1, ntp)
        def _(p):
            t = peer(p)
            to(rs_send.at[h, t], rs_got.at[h, me], rs_ssem.at[h, t], rs_rsem.at[h, me], (g, t)).start()

    load_o.wait()
    project(0, join(of_request(0), short_part))
    long = of_request(1)

    ask.wait_recv()
    top, total, out = cache_part(
        both_heads(guest_q[...]),
        kbuf[over(0, HALF)],
        vbuf[over(0, HALF)],
        slopes,
        lens[guest].astype(F32),
        1,
        2,
    )
    part_o[...] = out
    lane = lax.broadcasted_iota(jnp.int32, (2 * TREE, 128), 1)
    part_s[...] = jnp.where(lane < 64, top, total)
    give_o = to(part_o, back_o, pair_send.at[1], pair_recv.at[1], (partner, me))
    give_s = to(part_s, back_s, pair_send.at[2], pair_recv.at[2], (partner, me))
    give_o.start()
    give_s.start()

    long_part = cache_part(
        both_heads(tree[0, TREE : 2 * TREE]),
        kbuf[over(HALF, HALF)],
        vbuf[over(HALF, HALF)],
        slopes,
        lens[mine].astype(F32),
        0,
        2,
    )
    long = join(long, long_part)
    give_o.wait_recv()
    give_s.wait_recv()
    back = back_s[...]
    project(1, join(long, (back[:, 0:1], back[:, 64:65], back_o[...])))

    half_width = width // 2
    here = (mx, mz)

    def line(item, half, at, some=slice(None)):
        return spread.at[item, half, some, at] if half == 0 else spread.at[item, half, at, some]

    def moves(item, half, base, made):
        out = []
        for j, (sent, got, where) in enumerate(made):
            sems = ring_ssem.at[item, half, base + j], ring_rsem.at[item, half, base + j]
            out.append(
                (functools.partial(to, sent, sent, *sems, where), functools.partial(to, got, got, *sems, where))
            )
        return out

    def first_phase(item):
        out = []
        for half in range(2):
            made = []
            for by in (1, side - 1, 2):
                other = lax.rem(here[half] + side - by, side)
                x, z = (other, mz) if half == 0 else (mx, other)
                made.append((spread.at[item, half, mx, mz], spread.at[item, half, x, z], hop(half, by)))
            out += moves(item, half, 0, made)
        return out

    def second_phase(item):
        out = []
        for half in range(2):
            mid = here[1 - half]
            made = []
            for by in (1, side - 1):
                got = line(item, half, lax.rem(mid + side - by, side))
                made.append((line(item, half, mid), got, hop(1 - half, by)))
            out += moves(item, half, 3, made)
        return out

    def last_phase(item):
        out = []
        for half in range(2):
            mid = here[1 - half]
            opposite = lax.rem(mid + 2, side)
            made = []
            if item in ROUTED:
                made.append((line(item, half, mid), line(item, half, opposite), hop(1 - half, 2)))
            else:
                for by, some in ((1, pl.ds(0, side // 2)), (side - 1, pl.ds(side // 2, side // 2))):
                    sent = line(item, half, lax.rem(mid + side - by, side), some)
                    made.append((sent, line(item, half, opposite, some), hop(1 - half, by)))
            out += moves(item, half, 5, made)
        return out

    def follow(arrived, onward):
        for _, copy in arrived:
            copy().wait_recv()
        for copy, _ in onward:
            copy().start()

    def one_two(item):
        follow(first_phase(item), second_phase(item) + (last_phase(item) if item in ROUTED else []))

    def two_three(item):
        follow(second_phase(item), [] if item in ROUTED else last_phase(item))

    def publish(item, rows):
        rows = rows.astype(BF16)
        for half in range(2):
            spread[item, half, mx, mz] = rows[:, half * half_width : (half + 1) * half_width]
        follow((), first_phase(item))

    lane = lax.broadcasted_iota(jnp.int32, (TREE, 128), 1)

    def share_rows(h):
        def add_share(p, so_far):
            s = peer(p)
            to(rs_send.at[h, s], rs_got.at[h, s], rs_ssem.at[h, s], rs_rsem.at[h, s], (g, s)).wait_recv()
            return so_far + rs_got[h, s].astype(F32)

        hidden = residual[h * TREE : (h + 1) * TREE, :].astype(F32) + rs_send[h, me].astype(F32)
        hidden = lax.fori_loop(1, ntp, add_share, hidden)
        block_sum = jnp.sum(hidden, axis=1, keepdims=True)
        block_square = jnp.sum(hidden * hidden, axis=1, keepdims=True)
        block_mean = block_sum * (1.0 / width)
        square[0:TREE, :] = jnp.where(
            lane == 0, block_sum, jnp.where(lane == 1, block_square, jnp.where(lane == 2, block_mean, 0.0))
        )
        stat_got[h, me] = square[...].T[0:8]
        stat_got[h, me, 4:6, :] = gain[...]

        @pl.loop(1, ntp)
        def _(p):
            t = peer(p)
            stat = stat_got.at[h, me]
            to(stat, stat, stat_ssem.at[h, t], stat_rsem.at[h, me], (g, t)).start()

        publish(h, hidden - block_mean)

    def normalise(h):
        @pl.loop(1, ntp)
        def _(p):
            s = peer(p)
            stat = stat_got.at[h, s]
            to(stat, stat, stat_ssem.at[h, s], stat_rsem.at[h, s], (g, s)).wait_recv()

        follow(second_phase(h) + last_phase(h), ())

        stats = stat_got[h].reshape(128, 128).T[0:TREE]
        mean = jnp.sum(jnp.where(lane % 8 == 0, stats, 0.0), axis=1, keepdims=True) * (1.0 / D)
        squares = jnp.sum(jnp.where(lane % 8 == 1, stats, 0.0), axis=1, keepdims=True) * (1.0 / D)
        scale = lax.rsqrt(squares - mean * mean + EPSILON)
        for s in range(ntp):
            shift = stats[:, 8 * s + 2 : 8 * s + 3] - mean
            gains = jnp.concatenate([stat_got[h, s, 4:5, :], stat_got[h, s, 5:6, :]], axis=1)
            rows = jnp.concatenate([spread[h, half, s // side, s % side] for half in range(2)], axis=1)
            acts[h * TREE : (h + 1) * TREE, s * width : (s + 1) * width] = (
                (rows.astype(F32) + shift) * scale * gains
            ).astype(BF16)

    def draft(h, k):
        rows = slice(h * TREE, (h + 1) * TREE)
        update = dot(acts[rows, :], dw[k])
        own_rows = acts[rows, cols(me)].astype(F32)
        publish(2 + 2 * k + h, own_rows + update / (1.0 + jnp.exp(-update)))

    def item(h, k):
        return 2 + 2 * k + h

    share_rows(0)
    one_two(0)
    share_rows(1)
    one_two(1)
    normalise(0)
    load_d.wait()
    for k in range(DRAFTS):
        draft(0, k)
    one_two(item(0, 0))
    normalise(1)
    draft(1, 0)
    one_two(item(0, 1))
    draft(1, 1)
    draft(1, 2)
    one_two(item(0, 2))
    two_three(item(0, 0))

    square[...] = jnp.zeros_like(square)
    square[0:4, 0:tokens] = targets[...].astype(F32)
    wanted = square[...].T[0:tokens]

    load_w.wait()
    entry = (lax.broadcasted_iota(jnp.int32, (1, vocab), 1) + me * vocab).astype(F32)
    lane = lax.broadcasted_iota(jnp.int32, (tokens, 128), 1)

    def block(first, rows, at, n):
        logits[first : first + rows, pl.ds(at, n)] = dot_nt(acts[first : first + rows, :], vw[pl.ds(at, n), :])

    def tally(k, summary):
        x = logits[k * tokens : (k + 1) * tokens, :]
        top = jnp.max(x, axis=1, keepdims=True)
        total = jnp.sum(jnp.exp(x - top), axis=1, keepdims=True)
        picked = jnp.sum(jnp.where(entry == wanted[:, k : k + 1], x, 0.0), axis=1, keepdims=True)
        for c, value in enumerate((top, total, picked)):
            summary = jnp.where(lane == 8 * c + k, value, summary)
        return summary

    def base(first, last):
        step = 256
        for at in range(first * step, min(last * step, vocab), step):
            block(0, tokens, at, min(step, vocab - at))

    one_two(item(1, 0))
    two_three(item(0, 1))
    one_two(item(1, 1))
    base(0, 2)
    two_three(item(0, 2))
    one_two(item(1, 2))
    base(2, 8)
    summary = tally(0, jnp.zeros((tokens, 128), F32))

    for k in range(DRAFTS):
        for h in range(2):
            i = item(h, k)
            follow((second_phase(i) if i in ROUTED else []) + last_phase(i), ())
            at = (2 * (k + 1) + h) * TREE
            for s in range(ntp):
                acts[at : at + TREE, s * width : (s + 1) * width] = jnp.concatenate(
                    [spread[i, half, s // side, s % side] for half in range(2)], axis=1
                )

    step = STEP
    whole = vocab // step

    @pl.loop(0, whole)
    def _(i):
        block(tokens, DRAFTS * tokens, pl.multiple_of(i * step, step), step)

    if vocab > whole * step:
        block(tokens, DRAFTS * tokens, whole * step, vocab - whole * step)
    for k in range(1, DRAFTS + 1):
        summary = tally(k, summary)
    square[0:tokens, :] = summary
    fin_got[me] = square[...].T[0:24]

    @pl.loop(1, ntp)
    def _(p):
        t = peer(p)
        to(fin_got.at[me], fin_got.at[me], fin_ssem.at[t], fin_rsem.at[me], (g, t)).start()

    for i in range(2 * (DRAFTS + 1)):
        for copy, _ in first_phase(i) + second_phase(i) + last_phase(i):
            copy().wait_send()
    ask.wait_send()
    give_o.wait_send()
    give_s.wait_send()

    @pl.loop(1, ntp)
    def _(p):
        t = peer(p)
        for h in range(2):
            stat = stat_got.at[h, me]
            to(rs_send.at[h, t], rs_got.at[h, me], rs_ssem.at[h, t], rs_rsem.at[h, me], (g, t)).wait_send()
            to(stat, stat, stat_ssem.at[h, t], stat_rsem.at[h, me], (g, t)).wait_send()

    @pl.loop(1, ntp)
    def _(p):
        s = peer(p)
        to(fin_got.at[s], fin_got.at[s], fin_ssem.at[s], fin_rsem.at[s], (g, s)).wait_recv()

    tops, totals, picks = fin_got[:, 0:8, :], fin_got[:, 8:16, :], fin_got[:, 16:24, :]
    top = jnp.max(tops, axis=0)
    total = jnp.sum(totals * jnp.exp(tops - top[None]), axis=0)
    answer = jnp.sum(picks, axis=0) - (top + jnp.log(total))
    probs_out[...] = answer[0:4, 0:tokens]

    @pl.loop(1, ntp)
    def _(p):
        t = peer(p)
        to(fin_got.at[me], fin_got.at[me], fin_ssem.at[t], fin_rsem.at[me], (g, t)).wait_send()


def shards(ntp, *args):
    (
        residual,
        tree_qkv,
        kv_pool,
        page_table,
        cache_len,
        tree_parent,
        accepted_nodes,
        out_weight,
        norm_gain,
        draft_weight,
        vocab_weight,
        target_ids,
    ) = args
    tokens, width = residual.shape
    slots = kv_pool.shape[1]
    side = math.isqrt(ntp)
    used = (2 * HALF + SHORT_PAGES) * PAGE
    vmem = pl.BlockSpec(memory_space=pltpu.VMEM)
    smem = pl.BlockSpec(memory_space=pltpu.SMEM)
    anywhere = pl.BlockSpec(memory_space=pl.ANY)
    dma = pltpu.SemaphoreType.DMA
    return pl.pallas_call(
        functools.partial(kernel, ntp),
        out_shape=(
            jax.ShapeDtypeStruct((DRAFTS + 1, tokens), F32),
            jax.ShapeDtypeStruct((2, 8, width), BF16),
        ),
        in_specs=[vmem, vmem, anywhere, smem, smem, vmem, smem, anywhere, vmem, anywhere, anywhere, vmem],
        out_specs=(vmem, vmem),
        scratch_shapes=[
            pltpu.VMEM((slots, PAGE, width), BF16),
            pltpu.VMEM((slots, PAGE, width), BF16),
            pltpu.VMEM((used, width), BF16),
            pltpu.VMEM((used, width), BF16),
            pltpu.VMEM((width, D), BF16),
            pltpu.VMEM((DRAFTS, D, width), BF16),
            pltpu.VMEM(vocab_weight.shape, BF16),
            pltpu.VMEM((TREE, width), BF16),
            pltpu.VMEM((TREE, width), F32),
            pltpu.VMEM((2 * TREE, 128), F32),
            pltpu.VMEM((TREE, width), F32),
            pltpu.VMEM((2 * TREE, 128), F32),
            pltpu.VMEM((2, ntp, TREE, width), BF16),
            pltpu.VMEM((2, ntp, TREE, width), BF16),
            pltpu.VMEM((2, ntp, 8, 128), F32),
            pltpu.VMEM(((DRAFTS + 1) * tokens, D), BF16),
            pltpu.VMEM((2 * (DRAFTS + 1), 2, side, side, TREE, width // 2), BF16),
            pltpu.VMEM(((DRAFTS + 1) * tokens, vocab_weight.shape[0]), F32),
            pltpu.VMEM((ntp, 24, 128), F32),
            pltpu.VMEM((128, 128), F32),
            dma((5,)),
            dma((3,)),
            dma((3,)),
            dma((2, ntp)),
            dma((2, ntp)),
            dma((2, ntp)),
            dma((2, ntp)),
            dma((2 * (DRAFTS + 1), 2, 7)),
            dma((2 * (DRAFTS + 1), 2, 7)),
            dma((ntp,)),
            dma((ntp,)),
        ],
        compiler_params=pltpu.CompilerParams(
            collective_id=0, has_side_effects=True, vmem_limit_bytes=60 * 1024 * 1024
        ),
        cost_estimate=pl.CostEstimate(flops=6_200_000_000, bytes_accessed=27_000_000, transcendentals=1_000_000),
    )(
        residual,
        tree_qkv,
        kv_pool,
        page_table,
        cache_len,
        tree_parent,
        accepted_nodes,
        out_weight,
        norm_gain.reshape(2, width // 2),
        draft_weight,
        vocab_weight,
        target_ids,
    )


def solution(mesh):
    placed = (
        P("group", "tp"),
        P(None, "group", "tp"),
        P(None, "group", None, "tp"),
        P(),
        P(),
        P(),
        P("group", None),
        P("tp", None),
        P("tp"),
        P(None, None, "tp"),
        P("tp", None),
        P(None, "group"),
    )
    return jax.shard_map(
        functools.partial(shards, mesh.shape["tp"]),
        mesh=mesh,
        in_specs=placed,
        out_specs=(P(None, "group"), P(None, "group", "tp")),
        check_vma=False,
    )
```

```python
import functools
import math

import jax
import jax.numpy as jnp
from jax import lax
from jax.experimental import pallas as pl
from jax.experimental.pallas import tpu as pltpu
from jax.sharding import PartitionSpec as P

D = 4096
HEADS = 32
HD = 128
TREE = 48
SHORT_PAGES = 4
HALF = 14
PAGE = 128
DRAFTS = 3
EPSILON = 1e-05
STEP = 512
ROUTED = (0, 1, 3, 5, 7)
F32 = jnp.float32
BF16 = jnp.bfloat16
MESH = pl.DeviceIdType.MESH
NT = (((1,), (1,)), ((), ()))


def dot(a, b):
    return jnp.dot(a, b, preferred_element_type=F32)


def dot_nt(a, b):
    return lax.dot_general(a, b, NT, preferred_element_type=F32)


def both_heads(rows):
    lane = lax.broadcasted_iota(jnp.int32, rows.shape, 1)
    zero = jnp.zeros_like(rows)
    return jnp.concatenate(
        [jnp.where(lane < HD, rows, zero), jnp.where(lane >= HD, rows, zero)], axis=0
    )


def own_heads(stacked):
    n = stacked.shape[0] // 2
    return jnp.concatenate([stacked[:n, :HD], stacked[n:, HD:]], axis=1)


def wide(column):
    n = column.shape[0] // 2
    return jnp.concatenate(
        [jnp.broadcast_to(column[:n], (n, HD)), jnp.broadcast_to(column[n:], (n, HD))], axis=1
    )


def row_slopes(lane_index, rows):
    second = lax.broadcasted_iota(jnp.int32, (rows, 1), 0) >= rows // 2
    ordinal = (lane_index * 2 + 1 + jnp.where(second, 1, 0)).astype(F32)
    return jnp.exp2(-8.0 * ordinal / HEADS)


def cache_part(queries, keys, values, slopes, length, first, stride):
    span = keys.shape[0]
    rows = queries.shape[0] // 2
    index = lax.broadcasted_iota(jnp.int32, (1, span), 1)
    place = ((index >> 7) * stride + first) * PAGE + (index & (PAGE - 1))
    relative = place.astype(F32) - length
    exists = relative < 0.0
    bias = [jnp.where(exists, slopes[h * rows : h * rows + 1] * relative, -1e30) for h in range(2)]
    scores = dot_nt(queries, keys) * (1.0 / math.sqrt(HD))
    scores = jnp.concatenate([scores[:rows] + bias[0], scores[rows:] + bias[1]], axis=0)
    top = jnp.maximum(jnp.max(scores, axis=1, keepdims=True), -1e29)
    weights = jnp.exp(scores - top)
    total = jnp.sum(weights, axis=1, keepdims=True)
    return top, total, own_heads(dot(weights.astype(BF16), values))


def join(one, two):
    top = jnp.maximum(one[0], two[0])
    f1, f2 = jnp.exp(one[0] - top), jnp.exp(two[0] - top)
    return top, one[1] * f1 + two[1] * f2, one[2] * wide(f1) + two[2] * wide(f2)


def kernel(
    ntp,
    residual,
    tree,
    pool,
    pages,
    lens,
    parents,
    accepted,
    out_w,
    gain,
    draft_w,
    vocab_w,
    targets,
    probs_out,
    kept_out,
    kbank,
    vbank,
    kbuf,
    vbuf,
    ow,
    dw,
    vw,
    guest_q,
    part_o,
    part_s,
    back_o,
    back_s,
    rs_send,
    rs_got,
    stat_got,
    acts,
    spread,
    logits,
    fin_got,
    square,
    hbm_sem,
    pair_send,
    pair_recv,
    rs_ssem,
    rs_rsem,
    stat_ssem,
    stat_rsem,
    ring_ssem,
    ring_rsem,
    fin_ssem,
    fin_rsem,
):
    g = lax.axis_index("group")
    me = lax.axis_index("tp")
    partner = g + 1 - 2 * lax.rem(g, 2)
    tokens, width = residual.shape
    vocab = vw.shape[0]

    def peer(p):
        return lax.rem(me + p, ntp)

    def cols(t):
        return pl.ds(pl.multiple_of(t * width, width), width)

    side = math.isqrt(ntp)
    mx, mz = me // side, lax.rem(me, side)

    def hop(axis, by):
        if axis == 0:
            return (g, lax.rem(mx + by, side) * side + mz)
        return (g, mx * side + lax.rem(mz + by, side))

    def to(src, dst, ssem, rsem, where):
        return pltpu.make_async_remote_copy(
            src_ref=src, dst_ref=dst, send_sem=ssem, recv_sem=rsem, device_id=where, device_id_type=MESH
        )

    def load(src, dst, k):
        return pltpu.make_async_copy(src, dst, hbm_sem.at[k])

    load_k = load(pool.at[0], kbank, 0)
    load_v = load(pool.at[1], vbank, 1)
    load_o = load(out_w, ow, 2)
    load_d = load(draft_w, dw, 3)
    load_w = load(vocab_w, vw, 4)
    for copy in (load_k, load_v, load_o, load_d, load_w):
        copy.start()

    barrier = pltpu.get_barrier_semaphore()
    pl.semaphore_signal(barrier, inc=1, device_id=(partner, me), device_id_type=MESH)

    @pl.loop(1, ntp)
    def _(p):
        pl.semaphore_signal(barrier, inc=1, device_id=(g, peer(p)), device_id_type=MESH)

    parent = jnp.concatenate([parents[pl.ds(2 * g, 1), :], parents[pl.ds(2 * g + 1, 1), :]], axis=1)
    sub = lax.broadcasted_iota(jnp.int32, (tokens, tokens), 0)
    lan = lax.broadcasted_iota(jnp.int32, (tokens, tokens), 1)
    base = jnp.where(lan >= TREE, TREE, 0)
    linked = (parent + base == sub) & (lan != base)
    up = jnp.where(linked | (sub == lan), 1.0, 0.0).astype(BF16)
    for _ in range(TREE.bit_length()):
        up = jnp.minimum(dot(up, up), 1.0).astype(BF16)
    up32 = up.astype(F32)
    depth = jnp.sum(up32, axis=0, keepdims=True) - 1.0
    square[...] = jnp.zeros_like(square)
    square[0:tokens, 0:tokens] = up32
    ancestor = square[...].T[0:tokens, 0:tokens]

    row = lax.broadcasted_iota(jnp.int32, (16, tokens), 0)
    col = lax.broadcasted_iota(jnp.int32, (16, tokens), 1)
    pick = jnp.zeros((16, tokens), jnp.bool_)
    for i in range(8):
        pick = pick | ((row == i) & (col == (i // 4) * TREE + accepted[i // 4, i % 4]))
    chosen = jnp.where(pick, 1.0, 0.0).astype(BF16)
    for c in range(2):
        kept_out[c] = dot(chosen, tree[c + 1])[0:8].astype(BF16)

    pl.semaphore_wait(barrier, ntp)
    ask = to(tree.at[0, pl.ds(TREE, TREE)], guest_q, pair_send.at[0], pair_recv.at[0], (partner, me))
    ask.start()

    slopes = row_slopes(me, 2 * TREE)
    mine, guest = 2 * g + 1, 2 * partner + 1

    load_k.wait()

    def collect(bank, buf, start, count, request, first, stride):
        for i in range(count):
            buf[(start + i) * PAGE : (start + i + 1) * PAGE, :] = bank[pages[request, first + stride * i]]

    load_v.wait()
    for bank, buf in ((kbank, kbuf), (vbank, vbuf)):
        collect(bank, buf, 2 * HALF, SHORT_PAGES, 2 * g, 0, 1)

    def over(first, count):
        return pl.ds(first * PAGE, count * PAGE)

    short_part = cache_part(
        both_heads(tree[0, 0:TREE]),
        kbuf[over(2 * HALF, SHORT_PAGES)],
        vbuf[over(2 * HALF, SHORT_PAGES)],
        slopes,
        lens[2 * g].astype(F32),
        0,
        1,
    )

    seen = jnp.concatenate([ancestor, ancestor], axis=0) > 0.5
    scores = dot_nt(both_heads(tree[0]), tree[1]) * (1.0 / math.sqrt(HD))
    scores = jnp.where(seen, scores + row_slopes(me, 2 * tokens) * depth, -1e30)
    top = jnp.max(scores, axis=1, keepdims=True)
    weights = jnp.where(seen, jnp.exp(scores - top), 0.0)
    total = jnp.sum(weights, axis=1, keepdims=True)
    out = own_heads(dot(weights.astype(BF16), tree[2]))

    def of_request(r):
        at = r * TREE
        return (
            jnp.concatenate([top[at : at + TREE], top[tokens + at : tokens + at + TREE]], 0),
            jnp.concatenate([total[at : at + TREE], total[tokens + at : tokens + at + TREE]], 0),
            out[at : at + TREE],
        )

    def project(h, merged):
        attn = (merged[2] / wide(merged[1])).astype(BF16)
        for t in range(ntp):
            rs_send[h, t] = dot(attn, ow[:, t * width : (t + 1) * width]).astype(BF16)

        @pl.loop(1, ntp)
        def _(p):
            t = peer(p)
            to(rs_send.at[h, t], rs_got.at[h, me], rs_ssem.at[h, t], rs_rsem.at[h, me], (g, t)).start()

    load_o.wait()
    project(0, join(of_request(0), short_part))
    long = of_request(1)
    for bank, buf in ((kbank, kbuf), (vbank, vbuf)):
        collect(bank, buf, 0, HALF, guest, 1, 2)
        collect(bank, buf, HALF, HALF, mine, 0, 2)

    ask.wait_recv()
    top, total, out = cache_part(
        both_heads(guest_q[...]),
        kbuf[over(0, HALF)],
        vbuf[over(0, HALF)],
        slopes,
        lens[guest].astype(F32),
        1,
        2,
    )
    part_o[...] = out
    lane = lax.broadcasted_iota(jnp.int32, (2 * TREE, 128), 1)
    part_s[...] = jnp.where(lane < 64, top, total)
    give_o = to(part_o, back_o, pair_send.at[1], pair_recv.at[1], (partner, me))
    give_s = to(part_s, back_s, pair_send.at[2], pair_recv.at[2], (partner, me))
    give_o.start()
    give_s.start()

    long_part = cache_part(
        both_heads(tree[0, TREE : 2 * TREE]),
        kbuf[over(HALF, HALF)],
        vbuf[over(HALF, HALF)],
        slopes,
        lens[mine].astype(F32),
        0,
        2,
    )
    long = join(long, long_part)
    give_o.wait_recv()
    give_s.wait_recv()
    back = back_s[...]
    project(1, join(long, (back[:, 0:1], back[:, 64:65], back_o[...])))

    half_width = width // 2
    here = (mx, mz)

    def line(item, half, at, some=slice(None)):
        return spread.at[item, half, some, at] if half == 0 else spread.at[item, half, at, some]

    def moves(item, half, base, made):
        out = []
        for j, (sent, got, where) in enumerate(made):
            sems = ring_ssem.at[item, half, base + j], ring_rsem.at[item, half, base + j]
            out.append(
                (functools.partial(to, sent, sent, *sems, where), functools.partial(to, got, got, *sems, where))
            )
        return out

    def first_phase(item):
        out = []
        for half in range(2):
            made = []
            for by in (1, side - 1, 2):
                other = lax.rem(here[half] + side - by, side)
                x, z = (other, mz) if half == 0 else (mx, other)
                made.append((spread.at[item, half, mx, mz], spread.at[item, half, x, z], hop(half, by)))
            out += moves(item, half, 0, made)
        return out

    def second_phase(item):
        out = []
        for half in range(2):
            mid = here[1 - half]
            made = []
            for by in (1, side - 1):
                got = line(item, half, lax.rem(mid + side - by, side))
                made.append((line(item, half, mid), got, hop(1 - half, by)))
            out += moves(item, half, 3, made)
        return out

    def last_phase(item):
        out = []
        for half in range(2):
            mid = here[1 - half]
            opposite = lax.rem(mid + 2, side)
            made = []
            if item in ROUTED:
                made.append((line(item, half, mid), line(item, half, opposite), hop(1 - half, 2)))
            else:
                for by, some in ((1, pl.ds(0, side // 2)), (side - 1, pl.ds(side // 2, side // 2))):
                    sent = line(item, half, lax.rem(mid + side - by, side), some)
                    made.append((sent, line(item, half, opposite, some), hop(1 - half, by)))
            out += moves(item, half, 5, made)
        return out

    def follow(arrived, onward):
        for _, copy in arrived:
            copy().wait_recv()
        for copy, _ in onward:
            copy().start()

    def one_two(item):
        follow(first_phase(item), second_phase(item) + (last_phase(item) if item in ROUTED else []))

    def two_three(item):
        follow(second_phase(item), [] if item in ROUTED else last_phase(item))

    def publish(item, rows):
        rows = rows.astype(BF16)
        for half in range(2):
            spread[item, half, mx, mz] = rows[:, half * half_width : (half + 1) * half_width]
        follow((), first_phase(item))

    lane = lax.broadcasted_iota(jnp.int32, (TREE, 128), 1)

    def share_rows(h):
        def add_share(p, so_far):
            s = peer(p)
            to(rs_send.at[h, s], rs_got.at[h, s], rs_ssem.at[h, s], rs_rsem.at[h, s], (g, s)).wait_recv()
            return so_far + rs_got[h, s].astype(F32)

        hidden = residual[h * TREE : (h + 1) * TREE, :].astype(F32) + rs_send[h, me].astype(F32)
        hidden = lax.fori_loop(1, ntp, add_share, hidden)
        block_sum = jnp.sum(hidden, axis=1, keepdims=True)
        block_square = jnp.sum(hidden * hidden, axis=1, keepdims=True)
        block_mean = block_sum * (1.0 / width)
        square[0:TREE, :] = jnp.where(
            lane == 0, block_sum, jnp.where(lane == 1, block_square, jnp.where(lane == 2, block_mean, 0.0))
        )
        stat_got[h, me] = square[...].T[0:8]
        stat_got[h, me, 4:6, :] = gain[...]

        @pl.loop(1, ntp)
        def _(p):
            t = peer(p)
            stat = stat_got.at[h, me]
            to(stat, stat, stat_ssem.at[h, t], stat_rsem.at[h, me], (g, t)).start()

        publish(h, hidden - block_mean)

    def normalise(h):
        @pl.loop(1, ntp)
        def _(p):
            s = peer(p)
            stat = stat_got.at[h, s]
            to(stat, stat, stat_ssem.at[h, s], stat_rsem.at[h, s], (g, s)).wait_recv()

        follow(second_phase(h) + last_phase(h), ())

        stats = stat_got[h].reshape(128, 128).T[0:TREE]
        mean = jnp.sum(jnp.where(lane % 8 == 0, stats, 0.0), axis=1, keepdims=True) * (1.0 / D)
        squares = jnp.sum(jnp.where(lane % 8 == 1, stats, 0.0), axis=1, keepdims=True) * (1.0 / D)
        scale = lax.rsqrt(squares - mean * mean + EPSILON)
        for s in range(ntp):
            shift = stats[:, 8 * s + 2 : 8 * s + 3] - mean
            gains = jnp.concatenate([stat_got[h, s, 4:5, :], stat_got[h, s, 5:6, :]], axis=1)
            rows = jnp.concatenate([spread[h, half, s // side, s % side] for half in range(2)], axis=1)
            acts[h * TREE : (h + 1) * TREE, s * width : (s + 1) * width] = (
                (rows.astype(F32) + shift) * scale * gains
            ).astype(BF16)

    def draft(h, k):
        rows = slice(h * TREE, (h + 1) * TREE)
        update = dot(acts[rows, :], dw[k])
        own_rows = acts[rows, cols(me)].astype(F32)
        publish(2 + 2 * k + h, own_rows + update / (1.0 + jnp.exp(-update)))

    def item(h, k):
        return 2 + 2 * k + h

    share_rows(0)
    one_two(0)
    share_rows(1)
    one_two(1)
    normalise(0)
    load_d.wait()
    for k in range(DRAFTS):
        draft(0, k)
    one_two(item(0, 0))
    normalise(1)
    draft(1, 0)
    one_two(item(0, 1))
    draft(1, 1)
    draft(1, 2)
    one_two(item(0, 2))
    two_three(item(0, 0))

    square[...] = jnp.zeros_like(square)
    square[0:4, 0:tokens] = targets[...].astype(F32)
    wanted = square[...].T[0:tokens]

    load_w.wait()
    entry = (lax.broadcasted_iota(jnp.int32, (1, vocab), 1) + me * vocab).astype(F32)
    lane = lax.broadcasted_iota(jnp.int32, (tokens, 128), 1)

    def block(first, rows, at, n):
        logits[first : first + rows, pl.ds(at, n)] = dot_nt(acts[first : first + rows, :], vw[pl.ds(at, n), :])

    def tally(k, summary):
        x = logits[k * tokens : (k + 1) * tokens, :]
        top = jnp.max(x, axis=1, keepdims=True)
        total = jnp.sum(jnp.exp(x - top), axis=1, keepdims=True)
        picked = jnp.sum(jnp.where(entry == wanted[:, k : k + 1], x, 0.0), axis=1, keepdims=True)
        for c, value in enumerate((top, total, picked)):
            summary = jnp.where(lane == 8 * c + k, value, summary)
        return summary

    def base(first, last):
        step = 256
        for at in range(first * step, min(last * step, vocab), step):
            block(0, tokens, at, min(step, vocab - at))

    one_two(item(1, 0))
    two_three(item(0, 1))
    one_two(item(1, 1))
    one_two(item(1, 2))
    base(0, 1)
    two_three(item(0, 2))
    base(1, 8)
    summary = tally(0, jnp.zeros((tokens, 128), F32))

    for k in range(DRAFTS):
        for h in range(2):
            i = item(h, k)
            follow((second_phase(i) if i in ROUTED else []) + last_phase(i), ())
            at = (2 * (k + 1) + h) * TREE
            for s in range(ntp):
                acts[at : at + TREE, s * width : (s + 1) * width] = jnp.concatenate(
                    [spread[i, half, s // side, s % side] for half in range(2)], axis=1
                )

    step = STEP
    whole = vocab // step

    @pl.loop(0, whole)
    def _(i):
        block(tokens, DRAFTS * tokens, pl.multiple_of(i * step, step), step)

    if vocab > whole * step:
        block(tokens, DRAFTS * tokens, whole * step, vocab - whole * step)
    for k in range(1, DRAFTS + 1):
        summary = tally(k, summary)
    square[0:tokens, :] = summary
    fin_got[me] = square[...].T[0:24]

    @pl.loop(1, ntp)
    def _(p):
        t = peer(p)
        to(fin_got.at[me], fin_got.at[me], fin_ssem.at[t], fin_rsem.at[me], (g, t)).start()

    for i in range(2 * (DRAFTS + 1)):
        for copy, _ in first_phase(i) + second_phase(i) + last_phase(i):
            copy().wait_send()
    ask.wait_send()
    give_o.wait_send()
    give_s.wait_send()

    @pl.loop(1, ntp)
    def _(p):
        t = peer(p)
        for h in range(2):
            stat = stat_got.at[h, me]
            to(rs_send.at[h, t], rs_got.at[h, me], rs_ssem.at[h, t], rs_rsem.at[h, me], (g, t)).wait_send()
            to(stat, stat, stat_ssem.at[h, t], stat_rsem.at[h, me], (g, t)).wait_send()

    @pl.loop(1, ntp)
    def _(p):
        s = peer(p)
        to(fin_got.at[s], fin_got.at[s], fin_ssem.at[s], fin_rsem.at[s], (g, s)).wait_recv()

    tops, totals, picks = fin_got[:, 0:8, :], fin_got[:, 8:16, :], fin_got[:, 16:24, :]
    top = jnp.max(tops, axis=0)
    total = jnp.sum(totals * jnp.exp(tops - top[None]), axis=0)
    answer = jnp.sum(picks, axis=0) - (top + jnp.log(total))
    probs_out[...] = answer[0:4, 0:tokens]

    @pl.loop(1, ntp)
    def _(p):
        t = peer(p)
        to(fin_got.at[me], fin_got.at[me], fin_ssem.at[t], fin_rsem.at[me], (g, t)).wait_send()


def shards(ntp, *args):
    (
        residual,
        tree_qkv,
        kv_pool,
        page_table,
        cache_len,
        tree_parent,
        accepted_nodes,
        out_weight,
        norm_gain,
        draft_weight,
        vocab_weight,
        target_ids,
    ) = args
    tokens, width = residual.shape
    slots = kv_pool.shape[1]
    side = math.isqrt(ntp)
    used = (2 * HALF + SHORT_PAGES) * PAGE
    vmem = pl.BlockSpec(memory_space=pltpu.VMEM)
    smem = pl.BlockSpec(memory_space=pltpu.SMEM)
    anywhere = pl.BlockSpec(memory_space=pl.ANY)
    dma = pltpu.SemaphoreType.DMA
    return pl.pallas_call(
        functools.partial(kernel, ntp),
        out_shape=(
            jax.ShapeDtypeStruct((DRAFTS + 1, tokens), F32),
            jax.ShapeDtypeStruct((2, 8, width), BF16),
        ),
        in_specs=[vmem, vmem, anywhere, smem, smem, vmem, smem, anywhere, vmem, anywhere, anywhere, vmem],
        out_specs=(vmem, vmem),
        scratch_shapes=[
            pltpu.VMEM((slots, PAGE, width), BF16),
            pltpu.VMEM((slots, PAGE, width), BF16),
            pltpu.VMEM((used, width), BF16),
            pltpu.VMEM((used, width), BF16),
            pltpu.VMEM((width, D), BF16),
            pltpu.VMEM((DRAFTS, D, width), BF16),
            pltpu.VMEM(vocab_weight.shape, BF16),
            pltpu.VMEM((TREE, width), BF16),
            pltpu.VMEM((TREE, width), F32),
            pltpu.VMEM((2 * TREE, 128), F32),
            pltpu.VMEM((TREE, width), F32),
            pltpu.VMEM((2 * TREE, 128), F32),
            pltpu.VMEM((2, ntp, TREE, width), BF16),
            pltpu.VMEM((2, ntp, TREE, width), BF16),
            pltpu.VMEM((2, ntp, 8, 128), F32),
            pltpu.VMEM(((DRAFTS + 1) * tokens, D), BF16),
            pltpu.VMEM((2 * (DRAFTS + 1), 2, side, side, TREE, width // 2), BF16),
            pltpu.VMEM(((DRAFTS + 1) * tokens, vocab_weight.shape[0]), F32),
            pltpu.VMEM((ntp, 24, 128), F32),
            pltpu.VMEM((128, 128), F32),
            dma((5,)),
            dma((3,)),
            dma((3,)),
            dma((2, ntp)),
            dma((2, ntp)),
            dma((2, ntp)),
            dma((2, ntp)),
            dma((2 * (DRAFTS + 1), 2, 7)),
            dma((2 * (DRAFTS + 1), 2, 7)),
            dma((ntp,)),
            dma((ntp,)),
        ],
        compiler_params=pltpu.CompilerParams(
            collective_id=0, has_side_effects=True, vmem_limit_bytes=60 * 1024 * 1024
        ),
        cost_estimate=pl.CostEstimate(flops=6_200_000_000, bytes_accessed=27_000_000, transcendentals=1_000_000),
    )(
        residual,
        tree_qkv,
        kv_pool,
        page_table,
        cache_len,
        tree_parent,
        accepted_nodes,
        out_weight,
        norm_gain.reshape(2, width // 2),
        draft_weight,
        vocab_weight,
        target_ids,
    )


def solution(mesh):
    placed = (
        P("group", "tp"),
        P(None, "group", "tp"),
        P(None, "group", None, "tp"),
        P(),
        P(),
        P(),
        P("group", None),
        P("tp", None),
        P("tp"),
        P(None, None, "tp"),
        P("tp", None),
        P(None, "group"),
    )
    return jax.shard_map(
        functools.partial(shards, mesh.shape["tp"]),
        mesh=mesh,
        in_specs=placed,
        out_specs=(P(None, "group"), P(None, "group", "tp")),
        check_vma=False,
    )
```

```python
import functools
import math

import jax
import jax.numpy as jnp
from jax import lax
from jax.experimental import pallas as pl
from jax.experimental.pallas import tpu as pltpu
from jax.sharding import PartitionSpec as P

D = 4096
HEADS = 32
HD = 128
TREE = 48
SHORT_PAGES = 4
HALF = 14
PAGE = 128
DRAFTS = 3
EPSILON = 1e-05
STEP = 512
ROUTED = (0, 1, 5, 7)
F32 = jnp.float32
BF16 = jnp.bfloat16
MESH = pl.DeviceIdType.MESH
NT = (((1,), (1,)), ((), ()))


def dot(a, b):
    return jnp.dot(a, b, preferred_element_type=F32)


def dot_nt(a, b):
    return lax.dot_general(a, b, NT, preferred_element_type=F32)


def both_heads(rows):
    lane = lax.broadcasted_iota(jnp.int32, rows.shape, 1)
    zero = jnp.zeros_like(rows)
    return jnp.concatenate(
        [jnp.where(lane < HD, rows, zero), jnp.where(lane >= HD, rows, zero)], axis=0
    )


def own_heads(stacked):
    n = stacked.shape[0] // 2
    return jnp.concatenate([stacked[:n, :HD], stacked[n:, HD:]], axis=1)


def wide(column):
    n = column.shape[0] // 2
    return jnp.concatenate(
        [jnp.broadcast_to(column[:n], (n, HD)), jnp.broadcast_to(column[n:], (n, HD))], axis=1
    )


def row_slopes(lane_index, rows):
    second = lax.broadcasted_iota(jnp.int32, (rows, 1), 0) >= rows // 2
    ordinal = (lane_index * 2 + 1 + jnp.where(second, 1, 0)).astype(F32)
    return jnp.exp2(-8.0 * ordinal / HEADS)


def cache_part(queries, keys, values, slopes, length, first, stride):
    span = keys.shape[0]
    rows = queries.shape[0] // 2
    index = lax.broadcasted_iota(jnp.int32, (1, span), 1)
    place = ((index >> 7) * stride + first) * PAGE + (index & (PAGE - 1))
    relative = place.astype(F32) - length
    exists = relative < 0.0
    bias = [jnp.where(exists, slopes[h * rows : h * rows + 1] * relative, -1e30) for h in range(2)]
    scores = dot_nt(queries, keys) * (1.0 / math.sqrt(HD))
    scores = jnp.concatenate([scores[:rows] + bias[0], scores[rows:] + bias[1]], axis=0)
    top = jnp.maximum(jnp.max(scores, axis=1, keepdims=True), -1e29)
    weights = jnp.exp(scores - top)
    total = jnp.sum(weights, axis=1, keepdims=True)
    return top, total, own_heads(dot(weights.astype(BF16), values))


def join(one, two):
    top = jnp.maximum(one[0], two[0])
    f1, f2 = jnp.exp(one[0] - top), jnp.exp(two[0] - top)
    return top, one[1] * f1 + two[1] * f2, one[2] * wide(f1) + two[2] * wide(f2)


def kernel(
    ntp,
    residual,
    tree,
    pool,
    pages,
    lens,
    parents,
    accepted,
    out_w,
    gain,
    draft_w,
    vocab_w,
    targets,
    probs_out,
    kept_out,
    kbank,
    vbank,
    kbuf,
    vbuf,
    ow,
    dw,
    vw,
    guest_q,
    part_o,
    part_s,
    back_o,
    back_s,
    rs_send,
    rs_got,
    stat_got,
    acts,
    spread,
    logits,
    fin_got,
    square,
    hbm_sem,
    pair_send,
    pair_recv,
    rs_ssem,
    rs_rsem,
    stat_ssem,
    stat_rsem,
    ring_ssem,
    ring_rsem,
    fin_ssem,
    fin_rsem,
):
    g = lax.axis_index("group")
    me = lax.axis_index("tp")
    partner = g + 1 - 2 * lax.rem(g, 2)
    tokens, width = residual.shape
    vocab = vw.shape[0]

    def peer(p):
        return lax.rem(me + p, ntp)

    def cols(t):
        return pl.ds(pl.multiple_of(t * width, width), width)

    side = math.isqrt(ntp)
    mx, mz = me // side, lax.rem(me, side)

    def hop(axis, by):
        if axis == 0:
            return (g, lax.rem(mx + by, side) * side + mz)
        return (g, mx * side + lax.rem(mz + by, side))

    def to(src, dst, ssem, rsem, where):
        return pltpu.make_async_remote_copy(
            src_ref=src, dst_ref=dst, send_sem=ssem, recv_sem=rsem, device_id=where, device_id_type=MESH
        )

    def load(src, dst, k):
        return pltpu.make_async_copy(src, dst, hbm_sem.at[k])

    load_k = load(pool.at[0], kbank, 0)
    load_v = load(pool.at[1], vbank, 1)
    load_o = load(out_w, ow, 2)
    load_d = load(draft_w, dw, 3)
    load_w = load(vocab_w, vw, 4)
    for copy in (load_k, load_v, load_o, load_d, load_w):
        copy.start()

    barrier = pltpu.get_barrier_semaphore()
    pl.semaphore_signal(barrier, inc=1, device_id=(partner, me), device_id_type=MESH)

    @pl.loop(1, ntp)
    def _(p):
        pl.semaphore_signal(barrier, inc=1, device_id=(g, peer(p)), device_id_type=MESH)

    parent = jnp.concatenate([parents[pl.ds(2 * g, 1), :], parents[pl.ds(2 * g + 1, 1), :]], axis=1)
    sub = lax.broadcasted_iota(jnp.int32, (tokens, tokens), 0)
    lan = lax.broadcasted_iota(jnp.int32, (tokens, tokens), 1)
    base = jnp.where(lan >= TREE, TREE, 0)
    linked = (parent + base == sub) & (lan != base)
    up = jnp.where(linked | (sub == lan), 1.0, 0.0).astype(BF16)
    for _ in range(TREE.bit_length()):
        up = jnp.minimum(dot(up, up), 1.0).astype(BF16)
    up32 = up.astype(F32)
    depth = jnp.sum(up32, axis=0, keepdims=True) - 1.0
    square[...] = jnp.zeros_like(square)
    square[0:tokens, 0:tokens] = up32
    ancestor = square[...].T[0:tokens, 0:tokens]

    row = lax.broadcasted_iota(jnp.int32, (16, tokens), 0)
    col = lax.broadcasted_iota(jnp.int32, (16, tokens), 1)
    pick = jnp.zeros((16, tokens), jnp.bool_)
    for i in range(8):
        pick = pick | ((row == i) & (col == (i // 4) * TREE + accepted[i // 4, i % 4]))
    chosen = jnp.where(pick, 1.0, 0.0).astype(BF16)
    for c in range(2):
        kept_out[c] = dot(chosen, tree[c + 1])[0:8].astype(BF16)

    pl.semaphore_wait(barrier, ntp)
    ask = to(tree.at[0, pl.ds(TREE, TREE)], guest_q, pair_send.at[0], pair_recv.at[0], (partner, me))
    ask.start()

    slopes = row_slopes(me, 2 * TREE)
    mine, guest = 2 * g + 1, 2 * partner + 1

    load_k.wait()

    def collect(bank, buf, start, count, request, first, stride):
        for i in range(count):
            buf[(start + i) * PAGE : (start + i + 1) * PAGE, :] = bank[pages[request, first + stride * i]]

    load_v.wait()
    for bank, buf in ((kbank, kbuf), (vbank, vbuf)):
        collect(bank, buf, 2 * HALF, SHORT_PAGES, 2 * g, 0, 1)

    def over(first, count):
        return pl.ds(first * PAGE, count * PAGE)

    short_part = cache_part(
        both_heads(tree[0, 0:TREE]),
        kbuf[over(2 * HALF, SHORT_PAGES)],
        vbuf[over(2 * HALF, SHORT_PAGES)],
        slopes,
        lens[2 * g].astype(F32),
        0,
        1,
    )

    seen = jnp.concatenate([ancestor, ancestor], axis=0) > 0.5
    scores = dot_nt(both_heads(tree[0]), tree[1]) * (1.0 / math.sqrt(HD))
    scores = jnp.where(seen, scores + row_slopes(me, 2 * tokens) * depth, -1e30)
    top = jnp.max(scores, axis=1, keepdims=True)
    weights = jnp.where(seen, jnp.exp(scores - top), 0.0)
    total = jnp.sum(weights, axis=1, keepdims=True)
    out = own_heads(dot(weights.astype(BF16), tree[2]))

    def of_request(r):
        at = r * TREE
        return (
            jnp.concatenate([top[at : at + TREE], top[tokens + at : tokens + at + TREE]], 0),
            jnp.concatenate([total[at : at + TREE], total[tokens + at : tokens + at + TREE]], 0),
            out[at : at + TREE],
        )

    def project(h, merged):
        attn = (merged[2] / wide(merged[1])).astype(BF16)
        for t in range(ntp):
            rs_send[h, t] = dot(attn, ow[:, t * width : (t + 1) * width]).astype(BF16)

        @pl.loop(1, ntp)
        def _(p):
            t = peer(p)
            to(rs_send.at[h, t], rs_got.at[h, me], rs_ssem.at[h, t], rs_rsem.at[h, me], (g, t)).start()

    load_o.wait()
    project(0, join(of_request(0), short_part))
    long = of_request(1)
    for bank, buf in ((kbank, kbuf), (vbank, vbuf)):
        collect(bank, buf, 0, HALF, guest, 1, 2)
        collect(bank, buf, HALF, HALF, mine, 0, 2)

    ask.wait_recv()
    top, total, out = cache_part(
        both_heads(guest_q[...]),
        kbuf[over(0, HALF)],
        vbuf[over(0, HALF)],
        slopes,
        lens[guest].astype(F32),
        1,
        2,
    )
    part_o[...] = out
    lane = lax.broadcasted_iota(jnp.int32, (2 * TREE, 128), 1)
    part_s[...] = jnp.where(lane < 64, top, total)
    give_o = to(part_o, back_o, pair_send.at[1], pair_recv.at[1], (partner, me))
    give_s = to(part_s, back_s, pair_send.at[2], pair_recv.at[2], (partner, me))
    give_o.start()
    give_s.start()

    long_part = cache_part(
        both_heads(tree[0, TREE : 2 * TREE]),
        kbuf[over(HALF, HALF)],
        vbuf[over(HALF, HALF)],
        slopes,
        lens[mine].astype(F32),
        0,
        2,
    )
    long = join(long, long_part)
    give_o.wait_recv()
    give_s.wait_recv()
    back = back_s[...]
    project(1, join(long, (back[:, 0:1], back[:, 64:65], back_o[...])))

    half_width = width // 2
    here = (mx, mz)

    def line(item, half, at, some=slice(None)):
        return spread.at[item, half, some, at] if half == 0 else spread.at[item, half, at, some]

    def moves(item, half, base, made):
        out = []
        for j, (sent, got, where) in enumerate(made):
            sems = ring_ssem.at[item, half, base + j], ring_rsem.at[item, half, base + j]
            out.append(
                (functools.partial(to, sent, sent, *sems, where), functools.partial(to, got, got, *sems, where))
            )
        return out

    def first_phase(item):
        out = []
        for half in range(2):
            made = []
            for by in (1, side - 1, 2):
                other = lax.rem(here[half] + side - by, side)
                x, z = (other, mz) if half == 0 else (mx, other)
                made.append((spread.at[item, half, mx, mz], spread.at[item, half, x, z], hop(half, by)))
            out += moves(item, half, 0, made)
        return out

    def second_phase(item):
        out = []
        for half in range(2):
            mid = here[1 - half]
            made = []
            for by in (1, side - 1):
                got = line(item, half, lax.rem(mid + side - by, side))
                made.append((line(item, half, mid), got, hop(1 - half, by)))
            out += moves(item, half, 3, made)
        return out

    def last_phase(item):
        out = []
        for half in range(2):
            mid = here[1 - half]
            opposite = lax.rem(mid + 2, side)
            made = []
            if item in ROUTED:
                made.append((line(item, half, mid), line(item, half, opposite), hop(1 - half, 2)))
            else:
                for by, some in ((1, pl.ds(0, side // 2)), (side - 1, pl.ds(side // 2, side // 2))):
                    sent = line(item, half, lax.rem(mid + side - by, side), some)
                    made.append((sent, line(item, half, opposite, some), hop(1 - half, by)))
            out += moves(item, half, 5, made)
        return out

    def follow(arrived, onward):
        for _, copy in arrived:
            copy().wait_recv()
        for copy, _ in onward:
            copy().start()

    def one_two(item):
        follow(first_phase(item), second_phase(item) + (last_phase(item) if item in ROUTED else []))

    def two_three(item):
        follow(second_phase(item), [] if item in ROUTED else last_phase(item))

    def publish(item, rows):
        rows = rows.astype(BF16)
        for half in range(2):
            spread[item, half, mx, mz] = rows[:, half * half_width : (half + 1) * half_width]
        follow((), first_phase(item))

    lane = lax.broadcasted_iota(jnp.int32, (TREE, 128), 1)

    def share_rows(h):
        def add_share(p, so_far):
            s = peer(p)
            to(rs_send.at[h, s], rs_got.at[h, s], rs_ssem.at[h, s], rs_rsem.at[h, s], (g, s)).wait_recv()
            return so_far + rs_got[h, s].astype(F32)

        hidden = residual[h * TREE : (h + 1) * TREE, :].astype(F32) + rs_send[h, me].astype(F32)
        hidden = lax.fori_loop(1, ntp, add_share, hidden)
        block_sum = jnp.sum(hidden, axis=1, keepdims=True)
        block_square = jnp.sum(hidden * hidden, axis=1, keepdims=True)
        block_mean = block_sum * (1.0 / width)
        square[0:TREE, :] = jnp.where(
            lane == 0, block_sum, jnp.where(lane == 1, block_square, jnp.where(lane == 2, block_mean, 0.0))
        )
        stat_got[h, me] = square[...].T[0:8]
        stat_got[h, me, 4:6, :] = gain[...]

        @pl.loop(1, ntp)
        def _(p):
            t = peer(p)
            stat = stat_got.at[h, me]
            to(stat, stat, stat_ssem.at[h, t], stat_rsem.at[h, me], (g, t)).start()

        publish(h, hidden - block_mean)

    def normalise(h):
        @pl.loop(1, ntp)
        def _(p):
            s = peer(p)
            stat = stat_got.at[h, s]
            to(stat, stat, stat_ssem.at[h, s], stat_rsem.at[h, s], (g, s)).wait_recv()

        follow(second_phase(h) + last_phase(h), ())

        stats = stat_got[h].reshape(128, 128).T[0:TREE]
        mean = jnp.sum(jnp.where(lane % 8 == 0, stats, 0.0), axis=1, keepdims=True) * (1.0 / D)
        squares = jnp.sum(jnp.where(lane % 8 == 1, stats, 0.0), axis=1, keepdims=True) * (1.0 / D)
        scale = lax.rsqrt(squares - mean * mean + EPSILON)
        for s in range(ntp):
            shift = stats[:, 8 * s + 2 : 8 * s + 3] - mean
            gains = jnp.concatenate([stat_got[h, s, 4:5, :], stat_got[h, s, 5:6, :]], axis=1)
            rows = jnp.concatenate([spread[h, half, s // side, s % side] for half in range(2)], axis=1)
            acts[h * TREE : (h + 1) * TREE, s * width : (s + 1) * width] = (
                (rows.astype(F32) + shift) * scale * gains
            ).astype(BF16)

    def draft(h, k):
        rows = slice(h * TREE, (h + 1) * TREE)
        update = dot(acts[rows, :], dw[k])
        own_rows = acts[rows, cols(me)].astype(F32)
        publish(2 + 2 * k + h, own_rows + update / (1.0 + jnp.exp(-update)))

    def item(h, k):
        return 2 + 2 * k + h

    share_rows(0)
    one_two(0)
    share_rows(1)
    one_two(1)
    normalise(0)
    load_d.wait()
    for k in range(DRAFTS):
        draft(0, k)
    one_two(item(0, 0))
    normalise(1)
    draft(1, 0)
    one_two(item(0, 1))
    draft(1, 1)
    draft(1, 2)
    one_two(item(0, 2))
    two_three(item(0, 0))

    square[...] = jnp.zeros_like(square)
    square[0:4, 0:tokens] = targets[...].astype(F32)
    wanted = square[...].T[0:tokens]

    load_w.wait()
    entry = (lax.broadcasted_iota(jnp.int32, (1, vocab), 1) + me * vocab).astype(F32)
    lane = lax.broadcasted_iota(jnp.int32, (tokens, 128), 1)

    def block(first, rows, at, n):
        logits[first : first + rows, pl.ds(at, n)] = dot_nt(acts[first : first + rows, :], vw[pl.ds(at, n), :])

    def tally(k, summary):
        x = logits[k * tokens : (k + 1) * tokens, :]
        top = jnp.max(x, axis=1, keepdims=True)
        total = jnp.sum(jnp.exp(x - top), axis=1, keepdims=True)
        picked = jnp.sum(jnp.where(entry == wanted[:, k : k + 1], x, 0.0), axis=1, keepdims=True)
        for c, value in enumerate((top, total, picked)):
            summary = jnp.where(lane == 8 * c + k, value, summary)
        return summary

    def base(first, last):
        step = 256
        for at in range(first * step, min(last * step, vocab), step):
            block(0, tokens, at, min(step, vocab - at))

    one_two(item(1, 0))
    two_three(item(0, 1))
    one_two(item(1, 1))
    one_two(item(1, 2))
    base(0, 1)
    two_three(item(0, 2))
    base(1, 2)
    two_three(item(1, 0))
    base(2, 8)
    summary = tally(0, jnp.zeros((tokens, 128), F32))

    for k in range(DRAFTS):
        for h in range(2):
            i = item(h, k)
            follow((second_phase(i) if i in ROUTED else []) + last_phase(i), ())
            at = (2 * (k + 1) + h) * TREE
            for s in range(ntp):
                acts[at : at + TREE, s * width : (s + 1) * width] = jnp.concatenate(
                    [spread[i, half, s // side, s % side] for half in range(2)], axis=1
                )

    step = STEP
    whole = vocab // step

    @pl.loop(0, whole)
    def _(i):
        block(tokens, DRAFTS * tokens, pl.multiple_of(i * step, step), step)

    if vocab > whole * step:
        block(tokens, DRAFTS * tokens, whole * step, vocab - whole * step)
    for k in range(1, DRAFTS + 1):
        summary = tally(k, summary)
    square[0:tokens, :] = summary
    fin_got[me] = square[...].T[0:24]

    @pl.loop(1, ntp)
    def _(p):
        t = peer(p)
        to(fin_got.at[me], fin_got.at[me], fin_ssem.at[t], fin_rsem.at[me], (g, t)).start()

    for i in range(2 * (DRAFTS + 1)):
        for copy, _ in first_phase(i) + second_phase(i) + last_phase(i):
            copy().wait_send()
    ask.wait_send()
    give_o.wait_send()
    give_s.wait_send()

    @pl.loop(1, ntp)
    def _(p):
        t = peer(p)
        for h in range(2):
            stat = stat_got.at[h, me]
            to(rs_send.at[h, t], rs_got.at[h, me], rs_ssem.at[h, t], rs_rsem.at[h, me], (g, t)).wait_send()
            to(stat, stat, stat_ssem.at[h, t], stat_rsem.at[h, me], (g, t)).wait_send()

    @pl.loop(1, ntp)
    def _(p):
        s = peer(p)
        to(fin_got.at[s], fin_got.at[s], fin_ssem.at[s], fin_rsem.at[s], (g, s)).wait_recv()

    tops, totals, picks = fin_got[:, 0:8, :], fin_got[:, 8:16, :], fin_got[:, 16:24, :]
    top = jnp.max(tops, axis=0)
    total = jnp.sum(totals * jnp.exp(tops - top[None]), axis=0)
    answer = jnp.sum(picks, axis=0) - (top + jnp.log(total))
    probs_out[...] = answer[0:4, 0:tokens]

    @pl.loop(1, ntp)
    def _(p):
        t = peer(p)
        to(fin_got.at[me], fin_got.at[me], fin_ssem.at[t], fin_rsem.at[me], (g, t)).wait_send()


def shards(ntp, *args):
    (
        residual,
        tree_qkv,
        kv_pool,
        page_table,
        cache_len,
        tree_parent,
        accepted_nodes,
        out_weight,
        norm_gain,
        draft_weight,
        vocab_weight,
        target_ids,
    ) = args
    tokens, width = residual.shape
    slots = kv_pool.shape[1]
    side = math.isqrt(ntp)
    used = (2 * HALF + SHORT_PAGES) * PAGE
    vmem = pl.BlockSpec(memory_space=pltpu.VMEM)
    smem = pl.BlockSpec(memory_space=pltpu.SMEM)
    anywhere = pl.BlockSpec(memory_space=pl.ANY)
    dma = pltpu.SemaphoreType.DMA
    return pl.pallas_call(
        functools.partial(kernel, ntp),
        out_shape=(
            jax.ShapeDtypeStruct((DRAFTS + 1, tokens), F32),
            jax.ShapeDtypeStruct((2, 8, width), BF16),
        ),
        in_specs=[vmem, vmem, anywhere, smem, smem, vmem, smem, anywhere, vmem, anywhere, anywhere, vmem],
        out_specs=(vmem, vmem),
        scratch_shapes=[
            pltpu.VMEM((slots, PAGE, width), BF16),
            pltpu.VMEM((slots, PAGE, width), BF16),
            pltpu.VMEM((used, width), BF16),
            pltpu.VMEM((used, width), BF16),
            pltpu.VMEM((width, D), BF16),
            pltpu.VMEM((DRAFTS, D, width), BF16),
            pltpu.VMEM(vocab_weight.shape, BF16),
            pltpu.VMEM((TREE, width), BF16),
            pltpu.VMEM((TREE, width), F32),
            pltpu.VMEM((2 * TREE, 128), F32),
            pltpu.VMEM((TREE, width), F32),
            pltpu.VMEM((2 * TREE, 128), F32),
            pltpu.VMEM((2, ntp, TREE, width), BF16),
            pltpu.VMEM((2, ntp, TREE, width), BF16),
            pltpu.VMEM((2, ntp, 8, 128), F32),
            pltpu.VMEM(((DRAFTS + 1) * tokens, D), BF16),
            pltpu.VMEM((2 * (DRAFTS + 1), 2, side, side, TREE, width // 2), BF16),
            pltpu.VMEM(((DRAFTS + 1) * tokens, vocab_weight.shape[0]), F32),
            pltpu.VMEM((ntp, 24, 128), F32),
            pltpu.VMEM((128, 128), F32),
            dma((5,)),
            dma((3,)),
            dma((3,)),
            dma((2, ntp)),
            dma((2, ntp)),
            dma((2, ntp)),
            dma((2, ntp)),
            dma((2 * (DRAFTS + 1), 2, 7)),
            dma((2 * (DRAFTS + 1), 2, 7)),
            dma((ntp,)),
            dma((ntp,)),
        ],
        compiler_params=pltpu.CompilerParams(
            collective_id=0, has_side_effects=True, vmem_limit_bytes=60 * 1024 * 1024
        ),
        cost_estimate=pl.CostEstimate(flops=6_200_000_000, bytes_accessed=27_000_000, transcendentals=1_000_000),
    )(
        residual,
        tree_qkv,
        kv_pool,
        page_table,
        cache_len,
        tree_parent,
        accepted_nodes,
        out_weight,
        norm_gain.reshape(2, width // 2),
        draft_weight,
        vocab_weight,
        target_ids,
    )


def solution(mesh):
    placed = (
        P("group", "tp"),
        P(None, "group", "tp"),
        P(None, "group", None, "tp"),
        P(),
        P(),
        P(),
        P("group", None),
        P("tp", None),
        P("tp"),
        P(None, None, "tp"),
        P("tp", None),
        P(None, "group"),
    )
    return jax.shard_map(
        functools.partial(shards, mesh.shape["tp"]),
        mesh=mesh,
        in_specs=placed,
        out_specs=(P(None, "group"), P(None, "group", "tp")),
        check_vma=False,
    )
```
